32 devices in a mesh: ex: 8 (over z, x), feat: 4 (over y, core).
Axes of the slice: x: 2, y: 2, z: 4, core: 2. Of those that a mesh axis runs over, the one named last changes fastest.
Arguments:
- train_grads: bfloat16 [4096, 32768], P('ex', 'feat'), may hold values from -0.03125 to 0.03125
- audit_grads: bfloat16 [2, 8, 32, 32768], P(None, 'ex', None, 'feat'), may hold values from -6 to 6
- owner_map: int32 [16], replicated, may hold values from 0 to 15, as said below
- pair_blocks: int32 [8, 8], P('ex'), may hold values from 0 to 15, as said below
- pair_counts: int32 [8], P('ex'), may hold values from 1 to 8, as said below
Outputs:
- tiles: float32 [8, 8, 32, 512], P('ex', 'feat')
The draws below stay inside these ranges and needn't reach their ends.
Inputs may be any that keep to these rules, and one draw needn't show every extreme that they name: `owner_map`: a permutation of the audit blocks. `pair_blocks`: the 8 entries of each training block name audit blocks whose stored blocks lie on 8 different indices of ex (owner_map[a] % 8 differs); entries at or after pair_counts are not live. `pair_counts`: some training block has all 8 pairs live.
All inputs are finite; a program needn't handle non-finite values.
Results may differ from the reference program's by a relative error of at most 0.0003.
Values may be sent and summed in bfloat16 or wider, within the bound.
No kernel may reach another device: no remote copies, remote signals or barrier semaphores. Data moves between devices by JAX's collectives and lax.ppermute only.
A program may use at most 64 MiB of HBM per device.

```python
import jax
import jax.numpy as jnp
from jax import lax

F = 32768
TB = 512
AB = 32
ABLK_DEV = 2
NTB = 8
NAB = 16


def layout_tables(key):
    storage = jax.random.permutation(jax.random.fold_in(key, 11), NAB).astype(jnp.int32)
    inverse = jnp.argsort(storage).astype(jnp.int32)
    row_keys = jax.random.split(jax.random.fold_in(key, 12), NTB)

    def shuffle_row(row_key):
        return jax.random.permutation(row_key, NTB)
    owners = jax.vmap(shuffle_row)(row_keys).astype(jnp.int32)
    local = jax.random.randint(jax.random.fold_in(key, 13), (NTB, NTB), 0, ABLK_DEV, dtype=jnp.int32)
    pairs = jnp.take(inverse, local * NTB + owners)
    return (storage, pairs.astype(jnp.int32))


def draw_owner_map(key, part):
    storage, pairs = layout_tables(key)
    return storage


def draw_pair_blocks(key, part):
    storage, pairs = layout_tables(key)
    return pairs


def draw_pair_counts(key, part):
    first = jax.random.randint(jax.random.fold_in(key, 21), (NTB,), 1, NTB + 1, dtype=jnp.int32)
    second = jax.random.randint(jax.random.fold_in(key, 22), (NTB,), 1, NTB + 1, dtype=jnp.int32)
    counts = jnp.minimum(first, second)
    hottest = jax.random.randint(jax.random.fold_in(key, 23), (), 0, NTB, dtype=jnp.int32)
    return jnp.where(jnp.arange(NTB, dtype=jnp.int32) == hottest, NTB, counts).astype(jnp.int32)


def level_of(key, dims, shards, least, top_value):
    def one(position, shards_of):
        steps = jax.random.uniform(jax.random.fold_in(jax.random.fold_in(key, 6), position), (shards_of,), jnp.float32, least / len(shards), top_value / len(shards))
        return jnp.repeat(jnp.exp(steps), dims[position] // shards_of).reshape((-1,) + (1,) * (len(dims) - position - 1))

    level = one(*shards[0])
    for cut in shards[1:]:
        level = level * one(*cut)
    return level


def normal_values(key, extent, width, reach, cuts=(), kind=jnp.bfloat16):
    gain = level_of(key, extent, cuts, -0.22, 0.18) if cuts else 1.0
    result = jax.random.normal(key, extent, jnp.float32) * width * gain
    return jnp.minimum(jnp.maximum(result, -reach), reach).astype(kind)


def setup_inputs(seed: int = 0) -> dict:
    keys = jax.random.split(jax.random.key(seed), 6)
    return {
        "train_grads": normal_values(keys[0], (NTB * TB, F), F ** -0.5, 0.03125, ((0, 8), (1, 4))),
        "audit_grads": normal_values(keys[1], (ABLK_DEV, NTB, AB, F), 1.0, 6.0, ((1, 8), (3, 4))),
        "owner_map": draw_owner_map(jax.random.fold_in(keys[5], 71), 0),
        "pair_blocks": draw_pair_blocks(jax.random.fold_in(keys[5], 71), 0),
        "pair_counts": draw_pair_counts(jax.random.fold_in(keys[5], 71), 0),
    }


def reference(train_grads, audit_grads, owner_map, pair_blocks, pair_counts):
    blocks = train_grads.reshape(NTB, TB, F)
    order = jnp.arange(NTB, dtype=jnp.int32)

    def score_block(index):
        stored = jnp.take(owner_map, pair_blocks[index])
        rows = audit_grads[stored // NTB, stored % NTB]
        flat = rows.reshape(NTB * AB, F)
        scores = jnp.dot(flat, blocks[index].T, preferred_element_type=jnp.float32).reshape(NTB, AB, TB)
        live = (order < pair_counts[index]).astype(jnp.float32)
        return scores * live[:, None, None]

    return lax.map(score_block, jnp.arange(NTB, dtype=jnp.int32))
```

```python
import functools

import jax
import jax.numpy as jnp
from jax import lax
from jax.experimental import pallas as pl
from jax.experimental.pallas import tpu as pltpu
from jax.sharding import PartitionSpec as P

PAIR = 2
PARTS = 2


def matmul_kernel(rows_ref, train_ref, *rest):
    out_ref = rest[-1]

    @pl.when(pl.program_id(0) == 0)
    def _():
        out_ref[...] = rest[0][...] if len(rest) == 2 else jnp.zeros_like(out_ref)

    out_ref[...] += lax.dot_general(
        rows_ref[...], train_ref[...], (((1,), (1,)), ((), ())), preferred_element_type=jnp.float32
    )


def block_scores(rows, train, part, before):
    count, width = rows.shape
    examples = train.shape[0]
    step = min(width, 1024)
    steps = width // step
    whole = pl.BlockSpec((count, examples), lambda k: (0, 0))
    in_specs = [
        pl.BlockSpec((count, step), lambda k: (0, k)),
        pl.BlockSpec((examples, step), lambda k: (0, part * steps + k)),
    ]
    operands = [rows, train]
    if before is not None:
        in_specs.append(whole)
        operands.append(before)
    return pl.pallas_call(
        matmul_kernel,
        grid=(steps,),
        in_specs=in_specs,
        out_specs=whole,
        out_shape=jax.ShapeDtypeStruct((count, examples), jnp.float32),
        cost_estimate=pl.CostEstimate(
            flops=2 * count * examples * width,
            bytes_accessed=2 * (count + examples) * width + 4 * count * examples,
            transcendentals=0,
        ),
        compiler_params=pltpu.CompilerParams(vmem_limit_bytes=24 * 2**20),
    )(*operands)


def pick(blocks, index):
    return lax.dynamic_index_in_dim(blocks, index, 0, keepdims=False)


def shards(train_grads, audit_grads, owner_map, pair_blocks, pair_counts):
    peers = lax.axis_size("ex")
    feats = lax.axis_size("feat")
    chain = peers // PAIR
    me = lax.axis_index("ex")
    place, column = me // PAIR, me % PAIR
    own = audit_grads[:, 0]
    width = own.shape[-1] // PARTS
    across = [(i, i ^ 1) for i in range(peers)]
    upward = [(i, i + PAIR) for i in range(peers - PAIR)]
    downward = [(i + PAIR, i) for i in range(peers - PAIR)]

    stored = jnp.take(owner_map, pair_blocks[0])
    holder, local = stored % peers, stored // peers
    order = jnp.arange(peers, dtype=jnp.int32)
    wanted = jnp.sum(jnp.where(holder[None, :] == order[:, None], local[None, :], 0), axis=1)
    asked = lax.ppermute(wanted, "ex", across)

    above, below = {}, {}
    for h in range(PARTS):
        above[0, h] = below[0, h] = own[:, :, h * width : (h + 1) * width]
    for s in range(1, chain):
        for h in range(PARTS):
            below[s, h] = lax.ppermute(below[s - 1, h], "ex", upward)
            above[s, h] = lax.ppermute(above[s - 1, h], "ex", downward)

    short = jnp.minimum(place, chain - 1 - place)

    def nearest(j):
        paired = j <= 2 * short
        distance = jnp.where(paired, (j + 1) // 2, j - short)
        from_below = jnp.where(paired, j % 2 == 1, place > chain - 1 - place)
        return distance, from_below

    items = []
    items.append((place, [
        (pick(own, wanted[me])[:, h * width : (h + 1) * width],
         lax.ppermute(pick(own, asked[me])[:, h * width : (h + 1) * width], "ex", across))
        for h in range(PARTS)
    ]))
    for j in range(1, chain):
        distance, from_below = nearest(j)
        there = jnp.where(from_below, place - distance, place + distance)
        source = there * PAIR + column

        def arrived(h, index):
            result = None
            for d in sorted({(j + 1) // 2} | {j - m for m in range((j + 1) // 2)}):
                for table, side in ((below, from_below), (above, jnp.logical_not(from_below))):
                    block = pick(table[d, h], index)
                    result = block if result is None else jnp.where(
                        jnp.logical_and(side, distance == d), block, result)
            return result

        items.append((there, [
            (arrived(h, wanted[source]), lax.ppermute(arrived(h, asked[source]), "ex", across))
            for h in range(PARTS)
        ]))

    batches = [[0, 1]] + [[j] for j in range(2, chain)]
    scores, place_of = [], []
    for batch in batches:
        total = None
        for h in range(PARTS):
            rows = jnp.concatenate([r for j in batch for r in items[j][1][h]])
            total = block_scores(rows, train_grads, h, total)
        scores.append(total.reshape(len(batch) * PAIR, -1, total.shape[-1]))
        for j in batch:
            place_of += [items[j][0] * PAIR + column, items[j][0] * PAIR + (PAIR - 1 - column)]
    scores = jnp.concatenate(scores)
    where = jnp.sum(jnp.where(holder[:, None] == jnp.stack(place_of)[None, :], order[None, :], 0), axis=1)
    live = (order < pair_counts[0]).astype(jnp.float32)

    tiles = jnp.take(scores, where, axis=0) * live[:, None, None]
    f = lax.axis_index("feat")
    tiles = tiles.reshape(feats // 2, 2, peers // feats, *tiles.shape[1:])
    core = f % 2
    mine = lax.dynamic_index_in_dim(tiles, core, 1, keepdims=False)
    theirs = lax.dynamic_index_in_dim(tiles, 1 - core, 1, keepdims=False)
    mine = mine + lax.ppermute(theirs, "feat", [(i, i ^ 1) for i in range(feats)])
    half = feats // 2
    row = f // 2
    result = lax.dynamic_index_in_dim(mine, row, 0, keepdims=False)
    for k in range(1, half):
        to = (row + k) % half
        send = lax.dynamic_index_in_dim(mine, to, 0, keepdims=False)
        result = result + lax.ppermute(send, "feat", [(i, (i + 2 * k) % feats) for i in range(feats)])
    return result[None]


def solution(mesh):
    in_specs = (P("ex", "feat"), P(None, "ex", None, "feat"), P(), P("ex", None), P("ex"))
    out_specs = P("ex", "feat", None, None)
    return jax.shard_map(shards, mesh=mesh, in_specs=in_specs, out_specs=out_specs, check_vma=False)
```

```python
import functools

import jax
import jax.numpy as jnp
from jax import lax
from jax.experimental import pallas as pl
from jax.experimental.pallas import tpu as pltpu
from jax.sharding import PartitionSpec as P

PAIR = 2
PARTS = 2
STEP = 1024
SMALL_LIMIT = 8 * 2**20
VMEM_LIMIT = 48 * 2**20
COST = pl.CostEstimate(flops=10**9, bytes_accessed=8 * 2**20, transcendentals=0)
SMEM = pl.BlockSpec(memory_space=pltpu.SMEM)
VMEM = pl.BlockSpec(memory_space=pltpu.VMEM)
ANY = pl.BlockSpec(memory_space=pl.ANY)


def slots_of(chain):
    first = [(d, False) for d in range(1, chain - 1)]
    return [(0, False)] + first + [(d, True) for d in range((chain - 1) // 2, 0, -1)]


def plan_kernel(peers, me_ref, owner_ref, pairs_ref, counts_ref, wanted_ref, rows_ref):
    chain = peers // PAIR
    slots = len(slots_of(chain))
    me = me_ref[0]
    place, column = me // PAIR, lax.rem(me, PAIR)
    for k in range(peers):
        stored = owner_ref[pairs_ref[0, k]]
        holder = lax.rem(stored, peers)
        wanted_ref[holder] = stored // peers
        there = holder // PAIR
        far = jnp.abs(there - place)
        second = jnp.logical_and(there > place, place >= far)
        slot = jnp.where(far == chain - 1, slots - 1, jnp.where(second, slots - far, far))
        row = slot * PAIR + (lax.rem(holder, PAIR) != column).astype(jnp.int32)
        rows_ref[k] = jnp.where(k < counts_ref[0], row, -1)


def plan(me, owner_map, pair_blocks, pair_counts, peers):
    shape = jax.ShapeDtypeStruct((peers,), jnp.int32)
    return pl.pallas_call(
        functools.partial(plan_kernel, peers), in_specs=[SMEM] * 4, out_specs=[SMEM] * 2, out_shape=[shape] * 2
    )(me, owner_map, pair_blocks, pair_counts)


def relay_kernel(d, sides, me_ref, wanted_ref, asked_ref, *refs):
    sources, (mine_ref, theirs_ref, sems) = refs[: len(sides) * PARTS], refs[len(sides) * PARTS :]
    me = me_ref[0]
    place, column = me // PAIR, lax.rem(me, PAIR)
    for i, side in enumerate(sides):
        source = (place + side * d) * PAIR + column

        @pl.when((place >= d) == (side < 0))
        def _():
            copies = []
            for h in range(PARTS):
                ref = sources[i * PARTS + h]
                copies += [
                    pltpu.make_async_copy(ref.at[asked_ref[source]], theirs_ref.at[h], sems.at[2 * h]),
                    pltpu.make_async_copy(ref.at[wanted_ref[source]], mine_ref.at[h], sems.at[2 * h + 1]),
                ]
            for copy in copies:
                copy.start()
            for copy in copies:
                copy.wait()


def second_kernel(chain, d, me_ref, wanted_ref, asked_ref, *refs):
    sources, (mine_ref, theirs_ref, sems) = refs[:PARTS], refs[PARTS:]
    me = me_ref[0]
    source = jnp.minimum(me + d * PAIR, chain * PAIR - 1)
    copies = []
    for h, ref in enumerate(sources):
        copies += [
            pltpu.make_async_copy(ref.at[asked_ref[source]], theirs_ref.at[h], sems.at[2 * h]),
            pltpu.make_async_copy(ref.at[wanted_ref[source]], mine_ref.at[h], sems.at[2 * h + 1]),
        ]
    for copy in copies:
        copy.start()
    for copy in copies:
        copy.wait()


def relay(me, wanted, asked, above, below, d, second, chain):
    parts = range(PARTS)
    if second:
        kernel = functools.partial(second_kernel, chain, d)
        blocks = [above[d, h] for h in parts]
    else:
        kernel = functools.partial(relay_kernel, d, (-1, 1))
        blocks = [below[d, h] for h in parts] + [above[d, h] for h in parts]
    shape = jax.ShapeDtypeStruct((PARTS,) + blocks[0].shape[1:], blocks[0].dtype)
    return pl.pallas_call(
        kernel,
        in_specs=[SMEM] * 3 + [ANY] * len(blocks),
        out_specs=[VMEM] * 2,
        out_shape=[shape] * 2,
        scratch_shapes=[pltpu.SemaphoreType.DMA((2 * PARTS,))],
        cost_estimate=COST,
        compiler_params=pltpu.CompilerParams(vmem_limit_bytes=SMALL_LIMIT),
    )(me, wanted, asked, *blocks)


def own_kernel(me_ref, wanted_ref, asked_ref, own_ref, mine_ref, theirs_ref, sems):
    me = me_ref[0]
    width = mine_ref.shape[-1]
    copies = []
    for h in range(PARTS):
        at = slice(h * width, (h + 1) * width)
        copies += [
            pltpu.make_async_copy(own_ref.at[asked_ref[me], :, at], theirs_ref.at[h], sems.at[2 * h]),
            pltpu.make_async_copy(own_ref.at[wanted_ref[me], :, at], mine_ref.at[h], sems.at[2 * h + 1]),
        ]
    for copy in copies:
        copy.start()
    for copy in copies:
        copy.wait()


def relay_own(me, wanted, asked, own):
    shape = jax.ShapeDtypeStruct((PARTS, own.shape[1], own.shape[2] // PARTS), own.dtype)
    return pl.pallas_call(
        own_kernel,
        in_specs=[SMEM] * 3 + [ANY],
        out_specs=[VMEM] * 2,
        out_shape=[shape] * 2,
        scratch_shapes=[pltpu.SemaphoreType.DMA((2 * PARTS,))],
        cost_estimate=COST,
        compiler_params=pltpu.CompilerParams(vmem_limit_bytes=SMALL_LIMIT),
    )(me, wanted, asked, own)


def hand_kernel(chain, me_ref, notes_ref, above_ref, below_ref, out_ref, sems):
    me = me_ref[0]
    place, column = me // PAIR, lax.rem(me, PAIR)
    for ref, source in ((above_ref, (chain - 1) * PAIR + column), (below_ref, column)):

        @pl.when((place < chain // 2) == (source is not column))
        def _():
            copies = [
                pltpu.make_async_copy(ref.at[notes_ref[i, source]], out_ref.at[i], sems.at[i]) for i in range(PAIR)
            ]
            for copy in copies:
                copy.start()
            for copy in copies:
                copy.wait()


def hand(me, notes, above, below, chain):
    return pl.pallas_call(
        functools.partial(hand_kernel, chain),
        in_specs=[SMEM] * 2 + [ANY] * 2,
        out_specs=VMEM,
        out_shape=jax.ShapeDtypeStruct((PAIR,) + above.shape[1:], above.dtype),
        scratch_shapes=[pltpu.SemaphoreType.DMA((PAIR,))],
        cost_estimate=COST,
        compiler_params=pltpu.CompilerParams(vmem_limit_bytes=SMALL_LIMIT),
    )(me, notes, above, below)


def contract(rows, train):
    return lax.dot_general(rows, train, (((1,), (1,)), ((), ())), preferred_element_type=jnp.float32)


def scores_kernel(peers, feats, count, me_ref, rows_ref, *refs):
    blocks, refs = refs[:count], refs[count:]
    (far_refs, over_refs), refs = (refs[:PARTS], refs[PARTS : 2 * PARTS]), refs[2 * PARTS :]
    train_ref, keep_ref, give_ref, total_ref, rows_v, train_v, sems = refs
    _, size, width = blocks[0].shape
    step = min(width, STEP)
    chunks = [(h, at) for h in range(PARTS) for at in range(0, width, step)]
    place = me_ref[0] // PAIR
    end = jnp.logical_or(place == 0, place == peers // PAIR - 1)
    copies, near, away = [], [], []
    for i, (h, at) in enumerate(chunks):
        to = slice(h * width + at, h * width + at + step)
        train = pltpu.make_async_copy(train_ref.at[:, to], train_v.at[:, to], sems.at[i, count])
        rows = [
            pltpu.make_async_copy(
                ref.at[h, :, at : at + step], rows_v.at[b * size : (b + 1) * size, to], sems.at[i, b])
            for b, ref in enumerate(blocks)
        ]
        copies.append([train] + rows)
        near.append(rows[-PAIR:])
        away.append([
            pltpu.make_async_copy(
                ref.at[:, at : at + step], rows_v.at[b * size : (b + 1) * size, to], sems.at[i, b])
            for b, ref in ((count - PAIR, far_refs[h]), (count - PAIR + 1, over_refs[h]))
        ])
    for chunk in copies:
        for copy in chunk[:-PAIR]:
            copy.start()

    @pl.when(end)
    def _():
        for chunk in away:
            for copy in chunk:
                copy.start()

    @pl.when(jnp.logical_not(end))
    def _():
        for chunk in near:
            for copy in chunk:
                copy.start()

    for i, (chunk, (h, at)) in enumerate(zip(copies, chunks)):
        for copy in chunk:
            copy.wait()
        to = slice(h * width + at, h * width + at + step)
        value = lax.dot_general(
            rows_v[:, to], train_v[:, to], (((1,), (1,)), ((), ())), preferred_element_type=jnp.float32)
        total_ref[...] = value if i == 0 else total_ref[...] + value

    f = me_ref[1]
    core, line = lax.rem(f, 2), f // 2
    lines, each = feats // 2, peers // feats
    for away in range(lines):
        to = lax.rem(line + away, lines) * 2
        for i in range(each):
            for ref, c in ((keep_ref, core), (give_ref, 1 - core)):
                row = rows_ref[(to + c) * each + i]
                block = total_ref[pl.ds(pl.multiple_of(jnp.maximum(row, 0) * size, size), size), :]
                ref[away * each + i] = jnp.where(row >= 0, block, 0.0)


def pair_scores(me, rows, blocks, far, over, train, peers, feats):
    _, size, width = blocks[0].shape
    examples, features = train.shape
    count = len(blocks)
    return pl.pallas_call(
        functools.partial(scores_kernel, peers, feats, count),
        in_specs=[SMEM] * 2 + [ANY] * (count + 2 * PARTS + 1),
        out_specs=[VMEM] * 2,
        out_shape=[jax.ShapeDtypeStruct((peers // 2, size, examples), jnp.float32)] * 2,
        scratch_shapes=[
            pltpu.VMEM((count * size, examples), jnp.float32),
            pltpu.VMEM((count * size, features), train.dtype),
            pltpu.VMEM((examples, features), train.dtype),
            pltpu.SemaphoreType.DMA((PARTS * (width // min(width, STEP)), count + 1)),
        ],
        cost_estimate=pl.CostEstimate(
            flops=2 * count * size * examples * features,
            bytes_accessed=2 * (count * size + examples) * features,
            transcendentals=0,
        ),
        compiler_params=pltpu.CompilerParams(vmem_limit_bytes=VMEM_LIMIT),
    )(me, rows, *blocks, *far, *over, train)


def shards(train_grads, audit_grads, owner_map, pair_blocks, pair_counts):
    peers, feats = lax.axis_size("ex"), lax.axis_size("feat")
    chain = peers // PAIR
    me = jnp.stack([lax.axis_index("ex"), lax.axis_index("feat")]).astype(jnp.int32)
    own = audit_grads[:, 0]
    width = own.shape[-1] // PARTS
    parts = range(PARTS)
    across = [(i, i ^ 1) for i in range(peers)]
    upward = [(i, i + PAIR) for i in range(peers - PAIR)]
    downward = [(i + PAIR, i) for i in range(peers - PAIR)]
    reach = peers - PAIR
    ends = [(i, i + reach) for i in range(PAIR)] + [(i + reach, i) for i in range(PAIR)]

    half = [own[:, :, h * width : (h + 1) * width] for h in parts]
    above, below = {(0, h): half[h] for h in parts}, {(0, h): half[h] for h in parts}

    def along(s, h):
        below[s, h] = lax.ppermute(below[s - 1, h], "ex", upward[(s - 1) * PAIR :])
        above[s, h] = lax.ppermute(above[s - 1, h], "ex", downward[: len(downward) - (s - 1) * PAIR])

    for h in parts:
        along(1, h)
    below[1, 0], above[1, 0], pair_blocks = lax.optimization_barrier((below[1, 0], above[1, 0], pair_blocks))
    wanted, rows = plan(me, owner_map, pair_blocks, pair_counts, peers)
    asked = lax.ppermute(wanted, "ex", across)
    ends = [(i, i + PAIR) for i in range(PAIR)] + [(i, i - PAIR) for i in range(peers - PAIR, peers)]
    notes = lax.ppermute(jnp.stack([asked, wanted]), "ex", ends)
    for s in range(2, chain - 1):
        for h in parts:
            if s == 2 and h == PARTS - 1:
                below[1, h], above[1, h], notes = lax.optimization_barrier((below[1, h], above[1, h], notes))
            along(s, h)
    last = chain - 2

    sides = [(j, i) for i, j in ends]
    beyond = [i for i in across if not PAIR <= i[0] < peers - PAIR]
    far, over = [], []
    for h in parts:
        given = hand(me, notes, above[last, h], below[last, h], chain)
        if h < PARTS - 1:
            given = lax.ppermute(given, "ex", sides)
        else:
            given = [lax.ppermute(given[i], "ex", sides) for i in range(PAIR)]
        over.append(lax.ppermute(given[0], "ex", beyond))
        far.append(given[1])

    slots = slots_of(chain)
    blocks = {}
    for slot in slots:
        d, second = slot
        if d == 0:
            mine, theirs = relay_own(me, wanted, asked, own)
        else:
            mine, theirs = relay(me, wanted, asked, above, below, d, second, chain)
        other = [(i, j) for i, j in across if not second or d <= i // PAIR < chain - d]
        blocks[slot] = [mine, lax.ppermute(theirs, "ex", other)]

    blocks = [block for slot in slots for block in blocks[slot]]
    keep, give = pair_scores(me, rows, blocks, far, over, train_grads, peers, feats)

    total = keep + lax.ppermute(give, "feat", [(i, i ^ 1) for i in range(feats)])
    lines, each = feats // 2, peers // feats
    result = total[:each]
    for away in range(1, lines):
        send = total[away * each : (away + 1) * each]
        result = result + lax.ppermute(send, "feat", [(i, (i + 2 * away) % feats) for i in range(feats)])
    return result[None]


def solution(mesh):
    in_specs = (P("ex", "feat"), P(None, "ex", None, "feat"), P(), P("ex", None), P("ex"))
    out_specs = P("ex", "feat", None, None)
    return jax.shard_map(shards, mesh=mesh, in_specs=in_specs, out_specs=out_specs, check_vma=False)
```

```python
import functools

import jax
import jax.numpy as jnp
from jax import lax
from jax.experimental import pallas as pl
from jax.experimental.pallas import tpu as pltpu
from jax.sharding import PartitionSpec as P

PAIR = 2
PARTS = 2
STEP = 1024
SMALL_LIMIT = 8 * 2**20
VMEM_LIMIT = 52 * 2**20
COST = pl.CostEstimate(flops=0, bytes_accessed=0, transcendentals=0)
SMEM = pl.BlockSpec(memory_space=pltpu.SMEM)
VMEM = pl.BlockSpec(memory_space=pltpu.VMEM)
ANY = pl.BlockSpec(memory_space=pl.ANY)


def slots_of(chain):
    first = [(d, False) for d in range(1, chain - 1)]
    return [(0, False)] + first + [(d, True) for d in range((chain - 1) // 2, 0, -1)]


def plan_kernel(peers, owner_ref, pairs_ref, counts_ref, wanted_ref, rows_ref):
    chain = peers // PAIR
    slots = len(slots_of(chain))
    me = lax.axis_index("ex")
    place, column = me // PAIR, lax.rem(me, PAIR)
    lane = lax.broadcasted_iota(jnp.int32, (1, peers), 1)
    wanted, rows = jnp.zeros((1, peers), jnp.int32), jnp.zeros((1, peers), jnp.int32)
    for k in range(peers):
        stored = owner_ref[pairs_ref[0, k]]
        holder = lax.rem(stored, peers)
        wanted = jnp.where(lane == holder, stored // peers, wanted)
        there = holder // PAIR
        far = jnp.abs(there - place)
        second = jnp.logical_and(there > place, place >= far)
        slot = jnp.where(far == chain - 1, slots - 1, jnp.where(second, slots - far, far))
        row = slot * PAIR + (lax.rem(holder, PAIR) != column).astype(jnp.int32)
        rows = jnp.where(lane == k, jnp.where(k < counts_ref[0], row, -1), rows)
    wanted_ref[...] = wanted
    rows_ref[...] = rows


def plan(owner_map, pair_blocks, pair_counts, peers):
    shape = jax.ShapeDtypeStruct((1, peers), jnp.int32)
    return pl.pallas_call(
        functools.partial(plan_kernel, peers), in_specs=[SMEM] * 3, out_specs=[VMEM] * 2, out_shape=[shape] * 2
    )(owner_map, pair_blocks, pair_counts)


def relay_kernel(chain, d, count, wanted_ref, asked_ref, *refs):
    sources, outs, sems = refs[: -2 * count - 1], refs[-2 * count - 1 : -1], refs[-1]
    above_refs, below_refs = sources[:PARTS], sources[PARTS:]
    me = lax.axis_index("ex")
    place, column = me // PAIR, lax.rem(me, PAIR)

    def copies(j, blocks, source):
        made = []
        for h, ref in enumerate(blocks):
            made += [
                pltpu.make_async_copy(ref.at[asked_ref[0, source]], outs[2 * j + 1].at[h], sems.at[j, 2 * h]),
                pltpu.make_async_copy(ref.at[wanted_ref[0, source]], outs[2 * j].at[h], sems.at[j, 2 * h + 1]),
            ]
        return made

    up = copies(0, above_refs, jnp.minimum(place + d, chain - 1) * PAIR + column)
    waits = list(up)
    if below_refs:
        down = copies(0, below_refs, jnp.maximum(place - d, 0) * PAIR + column)

        @pl.when(place >= d)
        def _():
            for copy in down:
                copy.start()

        @pl.when(place < d)
        def _():
            for copy in up:
                copy.start()
    else:
        for copy in up:
            copy.start()
    if count > 1:
        waits += copies(1, above_refs, jnp.minimum(place + d, chain - 1) * PAIR + column)
        for copy in waits[len(up) :]:
            copy.start()
    for copy in waits:
        copy.wait()


def relay(wanted, asked, above, below, d, count, chain):
    blocks = [above[d, h] for h in range(PARTS)] + ([below[d, h] for h in range(PARTS)] if d else [])
    shape = jax.ShapeDtypeStruct((PARTS,) + blocks[0].shape[1:], blocks[0].dtype)
    return pl.pallas_call(
        functools.partial(relay_kernel, chain, d, count),
        in_specs=[SMEM] * 2 + [ANY] * len(blocks),
        out_specs=[VMEM] * (2 * count),
        out_shape=[shape] * (2 * count),
        scratch_shapes=[pltpu.SemaphoreType.DMA((count, 2 * PARTS))],
        cost_estimate=COST,
        compiler_params=pltpu.CompilerParams(vmem_limit_bytes=SMALL_LIMIT),
    )(wanted, asked, *blocks)


def cut_kernel(own_ref, *refs):
    outs, sems = refs[:-1], refs[-1]
    width = outs[0].shape[-1]
    copies = [
        pltpu.make_async_copy(own_ref.at[:, :, h * width : (h + 1) * width], out, sems.at[h])
        for h, out in enumerate(outs)
    ]
    for copy in copies:
        copy.start()
    for copy in copies:
        copy.wait()


def cut(own):
    shape = jax.ShapeDtypeStruct(own.shape[:2] + (own.shape[2] // PARTS,), own.dtype)
    return pl.pallas_call(
        cut_kernel,
        in_specs=[ANY],
        out_specs=[VMEM] * PARTS,
        out_shape=[shape] * PARTS,
        scratch_shapes=[pltpu.SemaphoreType.DMA((PARTS,))],
        cost_estimate=COST,
        compiler_params=pltpu.CompilerParams(vmem_limit_bytes=VMEM_LIMIT),
    )(own)


def hand_kernel(chain, notes_ref, above_ref, below_ref, *refs):
    outs, sems = refs[:-1], refs[-1]
    outs = [outs[0].at[i] for i in range(PAIR)] if len(outs) == 1 else outs
    me = lax.axis_index("ex")
    place, column = me // PAIR, lax.rem(me, PAIR)
    for ref, source, upper in ((above_ref, (chain - 1) * PAIR + column, False), (below_ref, column, True)):

        @pl.when((place >= chain // 2) == upper)
        def _():
            copies = [
                pltpu.make_async_copy(ref.at[notes_ref[i, source]], out, sems.at[i]) for i, out in enumerate(outs)
            ]
            for copy in copies:
                copy.start()
            for copy in copies:
                copy.wait()


def hand(notes, above, below, chain, stacked):
    shape = above.shape[1:]
    return pl.pallas_call(
        functools.partial(hand_kernel, chain),
        in_specs=[SMEM] + [ANY] * 2,
        out_specs=VMEM if stacked else [VMEM] * PAIR,
        out_shape=jax.ShapeDtypeStruct((PAIR,) + shape, above.dtype)
        if stacked
        else [jax.ShapeDtypeStruct(shape, above.dtype)] * PAIR,
        scratch_shapes=[pltpu.SemaphoreType.DMA((PAIR,))],
        cost_estimate=COST,
        compiler_params=pltpu.CompilerParams(vmem_limit_bytes=SMALL_LIMIT),
    )(notes, above, below)


def product_kernel(chain, full, last_parts, finish, *refs):
    blocks, refs = refs[:full], refs[full:]
    near_refs, refs = (refs[:PAIR], refs[PAIR:]) if last_parts else ((), refs)
    away_refs, refs = refs[: PAIR * len(last_parts)], refs[PAIR * len(last_parts) :]
    train_ref, refs = refs[0], refs[1:]
    rows_v, train_v, sems = refs[-3:]
    size, width = (blocks or near_refs)[0].shape[1:]
    step = min(width, STEP)
    place = lax.axis_index("ex") // PAIR
    end = jnp.logical_or(place == 0, place == chain - 1)
    chunks, near, away, starts = [], [], [], []
    for h in range(PARTS):
        if not full and h not in last_parts:
            continue
        for at in range(0, width, step):
            i = len(chunks)
            to = slice(h * width + at, h * width + at + step)

            def rows(b, source):
                return pltpu.make_async_copy(source, rows_v.at[b * size : (b + 1) * size, to], sems.at[i, b])

            copies = [pltpu.make_async_copy(train_ref.at[:, to], train_v.at[:, to], sems.at[i, full + PAIR])]
            copies += [rows(b, ref.at[h, :, at : at + step]) for b, ref in enumerate(blocks)]
            starts.append(list(copies))
            if h in last_parts:
                pair = away_refs[last_parts.index(h) * PAIR :][:PAIR]
                away.append([rows(full + b, ref.at[:, at : at + step]) for b, ref in enumerate(pair)])
                near.append([rows(full + b, ref.at[h, :, at : at + step]) for b, ref in enumerate(near_refs)])
                copies += near[-1]
            chunks.append((to, slice(0 if full else full * size, (full + PAIR * (h in last_parts)) * size), copies))

    @pl.when(end)
    def _():
        for copies in away:
            for copy in copies:
                copy.start()

    @pl.when(jnp.logical_not(end))
    def _():
        for copies in near:
            for copy in copies:
                copy.start()

    for copies in starts:
        for copy in copies:
            copy.start()

    if finish is None:
        total_ref, base = refs[0], 0
        total_ref[...] = jnp.zeros_like(total_ref)
    else:
        peers, feats, early = finish
        early_refs, (rows_ref, keep_ref, give_ref, total_ref, early_sems) = refs[:early], refs[early:-3]
        base = total_ref.shape[0] - PAIR * size
        copies, at = [], 0
        for i, ref in enumerate(early_refs):
            copies.append(pltpu.make_async_copy(ref, total_ref.at[at : at + ref.shape[0]], early_sems.at[i]))
            at += ref.shape[0]
        for copy in copies:
            copy.start()
        for copy in copies:
            copy.wait()

    for to, rows, copies in chunks:
        for copy in copies:
            copy.wait()
        total_ref[base + rows.start : base + rows.stop] += lax.dot_general(
            rows_v[rows, to], train_v[:, to], (((1,), (1,)), ((), ())), preferred_element_type=jnp.float32)
    if finish is None:
        return

    f = lax.axis_index("feat")
    core, line = lax.rem(f, 2), f // 2
    lines, each = feats // 2, peers // feats
    for away in range(lines):
        to = lax.rem(line + away, lines) * 2
        for i in range(each):
            for ref, c in ((keep_ref, core), (give_ref, 1 - core)):
                row = rows_ref[0, (to + c) * each + i]
                block = total_ref[pl.ds(pl.multiple_of(jnp.maximum(row, 0) * size, size), size), :]
                ref[away * each + i] = jnp.where(row >= 0, block, 0.0)


def product(blocks, last, away, train, chain, finish=None):
    size, width = last[0].shape[1:]
    examples, features = train.shape
    full, last_parts = len(blocks), sorted(away)
    operands = [*blocks, *(last if away else ()), *[a for h in last_parts for a in away[h]], train]
    count = (full + (PAIR if away else 0)) * size
    scratch = [
        pltpu.VMEM((count, features), train.dtype),
        pltpu.VMEM((examples, features), train.dtype),
        pltpu.SemaphoreType.DMA((PARTS * (width // min(width, STEP)), full + PAIR + 1)),
    ]
    in_specs = [ANY] * len(operands)
    if finish is None:
        out_shape, out_specs = jax.ShapeDtypeStruct((count, examples), jnp.float32), VMEM
        sizes = None
    else:
        peers, feats, early, rows = finish
        sizes = peers, feats, len(early)
        operands += [*early, rows]
        in_specs += [ANY] * len(early) + [SMEM]
        out_shape = [jax.ShapeDtypeStruct((peers // 2, size, examples), jnp.float32)] * 2
        out_specs = [VMEM] * 2
        scratch = [
            pltpu.VMEM((len(slots_of(chain)) * PAIR * size, examples), jnp.float32),
            pltpu.SemaphoreType.DMA((len(early),)),
        ] + scratch
    return pl.pallas_call(
        functools.partial(product_kernel, chain, full, last_parts, sizes),
        in_specs=in_specs,
        out_specs=out_specs,
        out_shape=out_shape,
        scratch_shapes=scratch,
        cost_estimate=COST,
        compiler_params=pltpu.CompilerParams(vmem_limit_bytes=VMEM_LIMIT),
    )(*operands)


def shards(train_grads, audit_grads, owner_map, pair_blocks, pair_counts):
    peers, feats = lax.axis_size("ex"), lax.axis_size("feat")
    chain = peers // PAIR
    own = audit_grads[:, 0]
    parts = range(PARTS)
    across = [(i, i ^ 1) for i in range(peers)]
    upward = [(i, i + PAIR) for i in range(peers - PAIR)]
    downward = [(i + PAIR, i) for i in range(peers - PAIR)]

    half = cut(own)
    above, below = {(0, h): half[h] for h in parts}, {(0, h): half[h] for h in parts}

    def along(s, h):
        below[s, h] = lax.ppermute(below[s - 1, h], "ex", upward[(s - 1) * PAIR :])
        above[s, h] = lax.ppermute(above[s - 1, h], "ex", downward[: len(downward) - (s - 1) * PAIR])

    for h in parts:
        along(1, h)
    wanted, rows = plan(owner_map, pair_blocks, pair_counts, peers)
    asked = lax.ppermute(wanted, "ex", across)
    ends = [(i, i + PAIR) for i in range(PAIR)] + [(i, i - PAIR) for i in range(peers - PAIR, peers)]
    notes = lax.ppermute(jnp.concatenate([wanted, asked]), "ex", ends)
    last = chain - 2

    slots = slots_of(chain)
    blocks = {}

    def hand_over(d):
        count = 1 + ((d, True) in slots)
        made = relay(wanted, asked, above, below, d, count, chain)
        for j in range(count):
            blocks[d, j > 0] = list(made[2 * j : 2 * j + 2])

    def receive(d):
        for second in (False, True):
            if (d, second) in slots:
                mine, theirs = blocks[d, second]
                if second:
                    theirs, blocks[d, False][1] = lax.optimization_barrier((theirs, blocks[d, False][1]))
                pairs = [(i, j) for i, j in across if not second or d <= i // PAIR < chain - d]
                blocks[d, second] = [mine, lax.ppermute(theirs, "ex", pairs)]

    hand_over(0)
    receive(0)
    hand_over(1)
    for s in range(2, chain - 1):
        for h in parts:
            if s == 2 and h == PARTS - 1:
                early = [slot for slot in slots if slot in blocks]
                gate = [blocks[slot][1] for slot in early]
                below[1, h], above[1, h], notes, gate = lax.optimization_barrier((below[1, h], above[1, h], notes, gate))
                for slot, block in zip(early, gate):
                    blocks[slot][1] = block
            along(s, h)
    receive(1)

    straight = [(j, i) for i, j in ends]
    diagonal = [(j, i ^ 1) for i, j in ends]
    beyond = [(i, j) for i, j in across if not PAIR <= i < peers - PAIR]
    both = [lax.ppermute(hand(notes, above[last, h], below[last, h], chain, True), "ex", straight) for h in parts[:-1]]
    mine, theirs = hand(notes, above[last, PARTS - 1], below[last, PARTS - 1], chain, False)
    both, mine, theirs = lax.optimization_barrier((both, mine, theirs))
    tail = {PARTS - 1: (lax.ppermute(mine, "ex", straight), lax.ppermute(theirs, "ex", diagonal))}
    away = {h: (b[0], lax.ppermute(b[1], "ex", beyond)) for h, b in enumerate(both)}

    for d in range(2, chain - 1):
        hand_over(d)
        receive(d)

    def scores(group, away, finish=None):
        return product([b for s in group for b in blocks[s]], blocks[slots[-1]], away, train_grads, chain, finish)

    early = [scores(slots[:2], {}), scores(slots[2:-1], away)]
    keep, give = scores([], tail, (peers, feats, early, rows))

    total = keep + lax.ppermute(give, "feat", [(i, i ^ 1) for i in range(feats)])
    lines, each = feats // 2, peers // feats
    result = total[:each]
    for away in range(1, lines):
        send = total[away * each : (away + 1) * each]
        result = result + lax.ppermute(send, "feat", [(i, (i + 2 * away) % feats) for i in range(feats)])
    return result[None]


def solution(mesh):
    in_specs = (P("ex", "feat"), P(None, "ex", None, "feat"), P(), P("ex", None), P("ex"))
    out_specs = P("ex", "feat", None, None)
    return jax.shard_map(shards, mesh=mesh, in_specs=in_specs, out_specs=out_specs, check_vma=False)
```

```python
import functools

import jax
import jax.numpy as jnp
from jax import lax
from jax.experimental import pallas as pl
from jax.experimental.pallas import tpu as pltpu
from jax.sharding import PartitionSpec as P

PAIR = 2
PARTS = 2
STEP = 1024
SMALL_LIMIT = 8 * 2**20
VMEM_LIMIT = 52 * 2**20
COST = pl.CostEstimate(flops=0, bytes_accessed=0, transcendentals=0)
SMEM = pl.BlockSpec(memory_space=pltpu.SMEM)
VMEM = pl.BlockSpec(memory_space=pltpu.VMEM)
ANY = pl.BlockSpec(memory_space=pl.ANY)


def slots_of(chain):
    first = [(d, False) for d in range(1, chain - 1)]
    return [(0, False)] + first + [(d, True) for d in range((chain - 1) // 2, 0, -1)]


def plan_kernel(peers, owner_ref, pairs_ref, counts_ref, wanted_ref, rows_ref):
    chain = peers // PAIR
    slots = len(slots_of(chain))
    me = lax.axis_index("ex")
    place, column = me // PAIR, lax.rem(me, PAIR)
    lane = lax.broadcasted_iota(jnp.int32, (1, peers), 1)
    wanted, rows = jnp.zeros((1, peers), jnp.int32), jnp.zeros((1, peers), jnp.int32)
    for k in range(peers):
        stored = owner_ref[pairs_ref[0, k]]
        holder = lax.rem(stored, peers)
        wanted = jnp.where(lane == holder, stored // peers, wanted)
        there = holder // PAIR
        far = jnp.abs(there - place)
        second = jnp.logical_and(there > place, place >= far)
        slot = jnp.where(far == chain - 1, slots - 1, jnp.where(second, slots - far, far))
        row = slot * PAIR + (lax.rem(holder, PAIR) != column).astype(jnp.int32)
        rows = jnp.where(lane == k, jnp.where(k < counts_ref[0], row, -1), rows)
    wanted_ref[...] = wanted
    rows_ref[...] = rows


def plan(owner_map, pair_blocks, pair_counts, peers):
    shape = jax.ShapeDtypeStruct((1, peers), jnp.int32)
    return pl.pallas_call(
        functools.partial(plan_kernel, peers), in_specs=[SMEM] * 3, out_specs=[VMEM] * 2, out_shape=[shape] * 2
    )(owner_map, pair_blocks, pair_counts)


def relay_kernel(chain, d, count, wanted_ref, asked_ref, *refs):
    sources, outs, sems = refs[: -2 * count - 1], refs[-2 * count - 1 : -1], refs[-1]
    above_refs, below_refs = sources[:PARTS], sources[PARTS:]
    me = lax.axis_index("ex")
    place, column = me // PAIR, lax.rem(me, PAIR)

    def copies(j, blocks, source):
        made = []
        for h, ref in enumerate(blocks):
            made += [
                pltpu.make_async_copy(ref.at[asked_ref[0, source]], outs[2 * j + 1].at[h], sems.at[j, 2 * h]),
                pltpu.make_async_copy(ref.at[wanted_ref[0, source]], outs[2 * j].at[h], sems.at[j, 2 * h + 1]),
            ]
        return made

    up = copies(0, above_refs, jnp.minimum(place + d, chain - 1) * PAIR + column)
    waits = list(up)
    if below_refs:
        down = copies(0, below_refs, jnp.maximum(place - d, 0) * PAIR + column)

        @pl.when(place >= d)
        def _():
            for copy in down:
                copy.start()

        @pl.when(place < d)
        def _():
            for copy in up:
                copy.start()
    else:
        for copy in up:
            copy.start()
    if count > 1:
        waits += copies(1, above_refs, jnp.minimum(place + d, chain - 1) * PAIR + column)
        for copy in waits[len(up) :]:
            copy.start()
    for copy in waits:
        copy.wait()


def relay(wanted, asked, above, below, d, count, chain):
    blocks = [above[d, h] for h in range(PARTS)] + ([below[d, h] for h in range(PARTS)] if d else [])
    shape = jax.ShapeDtypeStruct((PARTS,) + blocks[0].shape[1:], blocks[0].dtype)
    return pl.pallas_call(
        functools.partial(relay_kernel, chain, d, count),
        in_specs=[SMEM] * 2 + [ANY] * len(blocks),
        out_specs=[VMEM] * (2 * count),
        out_shape=[shape] * (2 * count),
        scratch_shapes=[pltpu.SemaphoreType.DMA((count, 2 * PARTS))],
        cost_estimate=COST,
        compiler_params=pltpu.CompilerParams(vmem_limit_bytes=SMALL_LIMIT),
    )(wanted, asked, *blocks)


def cut_kernel(own_ref, *refs):
    outs, sems = refs[:-1], refs[-1]
    width = outs[0].shape[-1]
    copies = [
        pltpu.make_async_copy(own_ref.at[:, :, h * width : (h + 1) * width], out, sems.at[h])
        for h, out in enumerate(outs)
    ]
    for copy in copies:
        copy.start()
    for copy in copies:
        copy.wait()


def cut(own):
    shape = jax.ShapeDtypeStruct(own.shape[:2] + (own.shape[2] // PARTS,), own.dtype)
    return pl.pallas_call(
        cut_kernel,
        in_specs=[ANY],
        out_specs=[VMEM] * PARTS,
        out_shape=[shape] * PARTS,
        scratch_shapes=[pltpu.SemaphoreType.DMA((PARTS,))],
        cost_estimate=COST,
        compiler_params=pltpu.CompilerParams(vmem_limit_bytes=VMEM_LIMIT),
    )(own)


def hand_kernel(chain, notes_ref, above_ref, below_ref, *refs):
    outs, sems = refs[:-1], refs[-1]
    outs = [outs[0].at[i] for i in range(PAIR)] if len(outs) == 1 else outs
    me = lax.axis_index("ex")
    place, column = me // PAIR, lax.rem(me, PAIR)
    for ref, source, upper in ((above_ref, (chain - 1) * PAIR + column, False), (below_ref, column, True)):

        @pl.when((place >= chain // 2) == upper)
        def _():
            copies = [
                pltpu.make_async_copy(ref.at[notes_ref[i, source]], out, sems.at[i]) for i, out in enumerate(outs)
            ]
            for copy in copies:
                copy.start()
            for copy in copies:
                copy.wait()


def hand(notes, above, below, chain, stacked):
    shape = above.shape[1:]
    return pl.pallas_call(
        functools.partial(hand_kernel, chain),
        in_specs=[SMEM] + [ANY] * 2,
        out_specs=VMEM if stacked else [VMEM] * PAIR,
        out_shape=jax.ShapeDtypeStruct((PAIR,) + shape, above.dtype)
        if stacked
        else [jax.ShapeDtypeStruct(shape, above.dtype)] * PAIR,
        scratch_shapes=[pltpu.SemaphoreType.DMA((PAIR,))],
        cost_estimate=COST,
        compiler_params=pltpu.CompilerParams(vmem_limit_bytes=SMALL_LIMIT),
    )(notes, above, below)


def product_kernel(chain, full, last_parts, finish, *refs):
    blocks, refs = refs[:full], refs[full:]
    near_refs, refs = (refs[:PAIR], refs[PAIR:]) if last_parts else ((), refs)
    away_refs, refs = refs[: PAIR * len(last_parts)], refs[PAIR * len(last_parts) :]
    train_ref, refs = refs[0], refs[1:]
    rows_v, train_v, sems = refs[-3:]
    size, width = (blocks or near_refs)[0].shape[1:]
    step = min(width, STEP)
    place = lax.axis_index("ex") // PAIR
    end = jnp.logical_or(place == 0, place == chain - 1)
    chunks, near, away, starts = [], [], [], []
    for h in range(PARTS):
        if not full and h not in last_parts:
            continue
        for at in range(0, width, step):
            i = len(chunks)
            to = slice(h * width + at, h * width + at + step)

            def rows(b, source):
                return pltpu.make_async_copy(source, rows_v.at[b * size : (b + 1) * size, to], sems.at[i, b])

            copies = [pltpu.make_async_copy(train_ref.at[:, to], train_v.at[:, to], sems.at[i, full + PAIR])]
            copies += [rows(b, ref.at[h, :, at : at + step]) for b, ref in enumerate(blocks)]
            starts.append(list(copies))
            if h in last_parts:
                pair = away_refs[last_parts.index(h) * PAIR :][:PAIR]
                away.append([rows(full + b, ref.at[:, at : at + step]) for b, ref in enumerate(pair)])
                near.append([rows(full + b, ref.at[h, :, at : at + step]) for b, ref in enumerate(near_refs)])
                copies += near[-1]
            chunks.append((to, slice(0 if full else full * size, (full + PAIR * (h in last_parts)) * size), copies))

    @pl.when(end)
    def _():
        for copies in away:
            for copy in copies:
                copy.start()

    @pl.when(jnp.logical_not(end))
    def _():
        for copies in near:
            for copy in copies:
                copy.start()

    for copies in starts:
        for copy in copies:
            copy.start()

    if finish is None:
        total_ref, base = refs[0], 0
        total_ref[...] = jnp.zeros_like(total_ref)
    else:
        peers, feats, early = finish
        early_refs, (rows_ref, keep_ref, give_ref, total_ref, early_sems) = refs[:early], refs[early:-3]
        base = total_ref.shape[0] - PAIR * size
        copies, at = [], 0
        for i, ref in enumerate(early_refs):
            copies.append(pltpu.make_async_copy(ref, total_ref.at[at : at + ref.shape[0]], early_sems.at[i]))
            at += ref.shape[0]
        for copy in copies:
            copy.start()
        for copy in copies:
            copy.wait()

    for to, rows, copies in chunks:
        for copy in copies:
            copy.wait()
        total_ref[base + rows.start : base + rows.stop] += lax.dot_general(
            rows_v[rows, to], train_v[:, to], (((1,), (1,)), ((), ())), preferred_element_type=jnp.float32)
    if finish is None:
        return

    f = lax.axis_index("feat")
    core, line = lax.rem(f, 2), f // 2
    lines, each = feats // 2, peers // feats
    for away in range(lines):
        to = lax.rem(line + away, lines) * 2
        for i in range(each):
            for ref, c in ((keep_ref, core), (give_ref, 1 - core)):
                row = rows_ref[0, (to + c) * each + i]
                block = total_ref[pl.ds(pl.multiple_of(jnp.maximum(row, 0) * size, size), size), :]
                ref[away * each + i] = jnp.where(row >= 0, block, 0.0)


def product(blocks, last, away, train, chain, finish=None):
    size, width = last[0].shape[1:]
    examples, features = train.shape
    full, last_parts = len(blocks), sorted(away)
    operands = [*blocks, *(last if away else ()), *[a for h in last_parts for a in away[h]], train]
    count = (full + (PAIR if away else 0)) * size
    scratch = [
        pltpu.VMEM((count, features), train.dtype),
        pltpu.VMEM((examples, features), train.dtype),
        pltpu.SemaphoreType.DMA((PARTS * (width // min(width, STEP)), full + PAIR + 1)),
    ]
    in_specs = [ANY] * len(operands)
    if finish is None:
        out_shape, out_specs = jax.ShapeDtypeStruct((count, examples), jnp.float32), VMEM
        sizes = None
    else:
        peers, feats, early, rows = finish
        sizes = peers, feats, len(early)
        operands += [*early, rows]
        in_specs += [ANY] * len(early) + [SMEM]
        out_shape = [jax.ShapeDtypeStruct((peers // 2, size, examples), jnp.float32)] * 2
        out_specs = [VMEM] * 2
        scratch = [
            pltpu.VMEM((len(slots_of(chain)) * PAIR * size, examples), jnp.float32),
            pltpu.SemaphoreType.DMA((len(early),)),
        ] + scratch
    return pl.pallas_call(
        functools.partial(product_kernel, chain, full, last_parts, sizes),
        in_specs=in_specs,
        out_specs=out_specs,
        out_shape=out_shape,
        scratch_shapes=scratch,
        cost_estimate=COST,
        compiler_params=pltpu.CompilerParams(vmem_limit_bytes=VMEM_LIMIT),
    )(*operands)


def shards(train_grads, audit_grads, owner_map, pair_blocks, pair_counts):
    peers, feats = lax.axis_size("ex"), lax.axis_size("feat")
    chain = peers // PAIR
    own = audit_grads[:, 0]
    parts = range(PARTS)
    across = [(i, i ^ 1) for i in range(peers)]
    upward = [(i, i + PAIR) for i in range(peers - PAIR)]
    downward = [(i + PAIR, i) for i in range(peers - PAIR)]

    half = cut(own)
    above, below = {(0, h): half[h] for h in parts}, {(0, h): half[h] for h in parts}

    def along(s, h):
        below[s, h] = lax.ppermute(below[s - 1, h], "ex", upward[(s - 1) * PAIR :])
        above[s, h] = lax.ppermute(above[s - 1, h], "ex", downward[: len(downward) - (s - 1) * PAIR])

    for h in parts:
        along(1, h)
    wanted, rows = plan(owner_map, pair_blocks, pair_counts, peers)
    asked = lax.ppermute(wanted, "ex", across)
    ends = [(i, i + PAIR) for i in range(PAIR)] + [(i, i - PAIR) for i in range(peers - PAIR, peers)]
    notes = lax.ppermute(jnp.concatenate([wanted, asked]), "ex", ends)
    last = chain - 2

    slots = slots_of(chain)
    blocks = {}

    def hand_over(d):
        count = 1 + ((d, True) in slots)
        made = relay(wanted, asked, above, below, d, count, chain)
        for j in range(count):
            blocks[d, j > 0] = list(made[2 * j : 2 * j + 2])

    def receive(d, after=()):
        for second in (False, True):
            if (d, second) in slots:
                mine, theirs = blocks[d, second]
                if second:
                    theirs, blocks[d, False][1], after = lax.optimization_barrier((theirs, blocks[d, False][1], after))
                pairs = [(i, j) for i, j in across if not second or d <= i // PAIR < chain - d]
                blocks[d, second] = [mine, lax.ppermute(theirs, "ex", pairs)]

    hand_over(0)
    receive(0)
    hand_over(1)
    for s in range(2, chain - 1):
        for h in parts:
            if s == 2 and h == PARTS - 1:
                early = [slot for slot in slots if slot in blocks]
                gate = [blocks[slot][1] for slot in early]
                below[1, h], above[1, h], notes, gate = lax.optimization_barrier((below[1, h], above[1, h], notes, gate))
                for slot, block in zip(early, gate):
                    blocks[slot][1] = block
            along(s, h)

    straight = [(j, i) for i, j in ends]
    diagonal = [(j, i ^ 1) for i, j in ends]
    beyond = [(i, j) for i, j in across if not PAIR <= i < peers - PAIR]
    away = {}
    for h in parts:
        up, down = above[last, h], below[last, h]
        if h > 0:
            mine, theirs = away[h - 1]
            up, down, theirs = lax.optimization_barrier((up, down, theirs))
            away[h - 1] = mine, theirs
        mine, theirs = hand(notes, up, down, chain, False)
        if h == 0:
            receive(1, (mine, theirs))
        away[h] = lax.ppermute(mine, "ex", straight), lax.ppermute(theirs, "ex", diagonal)
    tail = {PARTS - 1: away.pop(PARTS - 1)}

    for d in range(2, chain - 1):
        hand_over(d)
        receive(d)

    def scores(group, away, finish=None):
        return product([b for s in group for b in blocks[s]], blocks[slots[-1]], away, train_grads, chain, finish)

    early = [scores(slots[:2], {}), scores(slots[2:-1], away)]
    keep, give = scores([], tail, (peers, feats, early, rows))

    total = keep + lax.ppermute(give, "feat", [(i, i ^ 1) for i in range(feats)])
    lines, each = feats // 2, peers // feats
    result = total[:each]
    for away in range(1, lines):
        send = total[away * each : (away + 1) * each]
        result = result + lax.ppermute(send, "feat", [(i, (i + 2 * away) % feats) for i in range(feats)])
    return result[None]


def solution(mesh):
    in_specs = (P("ex", "feat"), P(None, "ex", None, "feat"), P(), P("ex", None), P("ex"))
    out_specs = P("ex", "feat", None, None)
    return jax.shard_map(shards, mesh=mesh, in_specs=in_specs, out_specs=out_specs, check_vma=False)
```

```python
import functools
import math

import jax
import jax.numpy as jnp
from jax import lax
from jax.experimental import pallas as pl
from jax.experimental.pallas import tpu as pltpu
from jax.sharding import PartitionSpec as P

PAIR = 2
PARTS = 2
EIGHTHS = 3
STEP = 1024
SMALL_LIMIT = 8 * 2**20
VMEM_LIMIT = 46 * 2**20
COST = pl.CostEstimate(flops=0, bytes_accessed=0, transcendentals=0)
SMEM = pl.BlockSpec(memory_space=pltpu.SMEM)
VMEM = pl.BlockSpec(memory_space=pltpu.VMEM)
ANY = pl.BlockSpec(memory_space=pl.ANY)


def cuts_of(features):
    return 0, features - features * EIGHTHS // 8, features


def slots_of(chain):
    first = [(d, False) for d in range(1, chain - 1)]
    return [(0, False)] + first + [(d, True) for d in range((chain - 1) // 2, 0, -1)]


def plan_kernel(peers, owner_ref, pairs_ref, counts_ref, wanted_ref, rows_ref):
    chain = peers // PAIR
    slots = len(slots_of(chain))
    me = lax.axis_index("ex")
    place, column = me // PAIR, lax.rem(me, PAIR)
    lane = lax.broadcasted_iota(jnp.int32, (1, peers), 1)
    wanted, rows = jnp.zeros((1, peers), jnp.int32), jnp.zeros((1, peers), jnp.int32)
    for k in range(peers):
        stored = owner_ref[pairs_ref[0, k]]
        holder = lax.rem(stored, peers)
        wanted = jnp.where(lane == holder, stored // peers, wanted)
        there = holder // PAIR
        far = jnp.abs(there - place)
        second = jnp.logical_and(there > place, place >= far)
        slot = jnp.where(far == chain - 1, slots - 1, jnp.where(second, slots - far, far))
        row = slot * PAIR + (lax.rem(holder, PAIR) != column).astype(jnp.int32)
        rows = jnp.where(lane == k, jnp.where(k < counts_ref[0], row, -1), rows)
    wanted_ref[...] = wanted
    rows_ref[...] = rows


def plan(owner_map, pair_blocks, pair_counts, peers):
    shape = jax.ShapeDtypeStruct((1, peers), jnp.int32)
    return pl.pallas_call(
        functools.partial(plan_kernel, peers), in_specs=[SMEM] * 3, out_specs=[VMEM] * 2, out_shape=[shape] * 2
    )(owner_map, pair_blocks, pair_counts)


def relay_kernel(chain, d, count, wants_ref, *refs):
    sources, outs, sems = refs[: -2 * count - 1], refs[-2 * count - 1 : -1], refs[-1]
    above_refs, below_refs = sources[:PARTS], sources[PARTS:]
    me = lax.axis_index("ex")
    place, column = me // PAIR, lax.rem(me, PAIR)

    def copies(j, blocks, source):
        made = []
        cuts = cuts_of(outs[0].shape[-1])
        for h, ref in enumerate(blocks):
            at = slice(cuts[h], cuts[h + 1])
            made += [
                pltpu.make_async_copy(ref.at[wants_ref[1, source]], outs[2 * j + 1].at[:, at], sems.at[j, 2 * h]),
                pltpu.make_async_copy(ref.at[wants_ref[0, source]], outs[2 * j].at[:, at], sems.at[j, 2 * h + 1]),
            ]
        return made

    up = copies(0, above_refs, jnp.minimum(place + d, chain - 1) * PAIR + column)
    waits = list(up)
    if below_refs:
        down = copies(0, below_refs, jnp.maximum(place - d, 0) * PAIR + column)

        @pl.when(place >= d)
        def _():
            for copy in down:
                copy.start()

        @pl.when(place < d)
        def _():
            for copy in up:
                copy.start()
    else:
        for copy in up:
            copy.start()
    if count > 1:
        waits += copies(1, above_refs, jnp.minimum(place + d, chain - 1) * PAIR + column)
        for copy in waits[len(up) :]:
            copy.start()
    for copy in waits:
        copy.wait()


def relay(wants, above, below, d, count, chain):
    blocks = [above[d, h] for h in range(PARTS)] + ([below[d, h] for h in range(PARTS)] if d else [])
    features = sum(b.shape[2] for b in blocks[:PARTS])
    shape = jax.ShapeDtypeStruct((blocks[0].shape[1], features), blocks[0].dtype)
    return pl.pallas_call(
        functools.partial(relay_kernel, chain, d, count),
        in_specs=[SMEM] + [ANY] * len(blocks),
        out_specs=[VMEM] * (2 * count),
        out_shape=[shape] * (2 * count),
        scratch_shapes=[pltpu.SemaphoreType.DMA((count, 2 * PARTS))],
        cost_estimate=COST,
        compiler_params=pltpu.CompilerParams(vmem_limit_bytes=SMALL_LIMIT),
    )(wants, *blocks)


def cut_kernel(own_ref, *refs):
    outs, sems = refs[:-1], refs[-1]
    cuts = cuts_of(own_ref.shape[-1])
    copies = [
        pltpu.make_async_copy(own_ref.at[:, :, cuts[h] : cuts[h + 1]], out, sems.at[h]) for h, out in enumerate(outs)
    ]
    for copy in copies:
        copy.start()
    for copy in copies:
        copy.wait()


def cut(own):
    cuts = cuts_of(own.shape[2])
    return pl.pallas_call(
        cut_kernel,
        in_specs=[ANY],
        out_specs=[VMEM] * PARTS,
        out_shape=[
            jax.ShapeDtypeStruct(own.shape[:2] + (stop - start,), own.dtype) for start, stop in zip(cuts, cuts[1:])
        ],
        scratch_shapes=[pltpu.SemaphoreType.DMA((PARTS,))],
        cost_estimate=COST,
        compiler_params=pltpu.CompilerParams(vmem_limit_bytes=VMEM_LIMIT),
    )(own)


def hand_kernel(chain, notes_ref, above_ref, below_ref, *refs):
    outs, sems = refs[:-1], refs[-1]
    outs = [outs[0].at[i] for i in range(PAIR)] if len(outs) == 1 else outs
    me = lax.axis_index("ex")
    place, column = me // PAIR, lax.rem(me, PAIR)
    for ref, source, upper in ((above_ref, (chain - 1) * PAIR + column, False), (below_ref, column, True)):

        @pl.when((place >= chain // 2) == upper)
        def _():
            copies = [
                pltpu.make_async_copy(ref.at[notes_ref[i, source]], out, sems.at[i]) for i, out in enumerate(outs)
            ]
            for copy in copies:
                copy.start()
            for copy in copies:
                copy.wait()


def hand(notes, above, below, chain, stacked):
    shape = above.shape[1:]
    return pl.pallas_call(
        functools.partial(hand_kernel, chain),
        in_specs=[SMEM] + [ANY] * 2,
        out_specs=VMEM if stacked else [VMEM] * PAIR,
        out_shape=jax.ShapeDtypeStruct((PAIR,) + shape, above.dtype)
        if stacked
        else [jax.ShapeDtypeStruct(shape, above.dtype)] * PAIR,
        scratch_shapes=[pltpu.SemaphoreType.DMA((PAIR,))],
        cost_estimate=COST,
        compiler_params=pltpu.CompilerParams(vmem_limit_bytes=SMALL_LIMIT),
    )(notes, above, below)


def product_kernel(chain, full, last_parts, finish, *refs):
    blocks, refs = refs[:full], refs[full:]
    near_refs, refs = (refs[:PAIR], refs[PAIR:]) if last_parts else ((), refs)
    away_refs, refs = refs[: PAIR * len(last_parts)], refs[PAIR * len(last_parts) :]
    train_ref, refs = refs[0], refs[1:]
    rows_v, train_v, sems = refs[-3:]
    size, features = (blocks or near_refs)[0].shape
    cuts = cuts_of(features)
    place = lax.axis_index("ex") // PAIR
    end = jnp.logical_or(place == 0, place == chain - 1)
    chunks, near, away, starts = [], [], [], []
    for h in range(PARTS):
        if not full and h not in last_parts:
            continue
        step = math.gcd(cuts[h + 1] - cuts[h], STEP)
        for at in range(cuts[h], cuts[h + 1], step):
            i = len(chunks)
            to = slice(at, at + step)

            def rows(b, source):
                return pltpu.make_async_copy(source, rows_v.at[b * size : (b + 1) * size, to], sems.at[i, b])

            copies = [pltpu.make_async_copy(train_ref.at[:, to], train_v.at[:, to], sems.at[i, full + PAIR])]
            copies += [rows(b, ref.at[:, to]) for b, ref in enumerate(blocks)]
            starts.append(list(copies))
            if h in last_parts:
                pair = away_refs[last_parts.index(h) * PAIR :][:PAIR]
                of_part = slice(at - cuts[h], at - cuts[h] + step)
                away.append([rows(full + b, ref.at[:, of_part]) for b, ref in enumerate(pair)])
                near.append([rows(full + b, ref.at[:, to]) for b, ref in enumerate(near_refs)])
                copies += near[-1]
            chunks.append((to, slice(0 if full else full * size, (full + PAIR * (h in last_parts)) * size), copies))

    @pl.when(end)
    def _():
        for copies in away:
            for copy in copies:
                copy.start()

    @pl.when(jnp.logical_not(end))
    def _():
        for copies in near:
            for copy in copies:
                copy.start()

    for copies in starts:
        for copy in copies:
            copy.start()

    if finish is None:
        total_ref, base = refs[0], 0
        total_ref[...] = jnp.zeros_like(total_ref)
    else:
        peers, feats = finish
        early_ref, rows_ref, keep_ref, give_ref, total_ref, early_sems = refs[:-3]
        last = total_ref.shape[0] - PAIR * size
        base = last - full * size
        copies = [
            pltpu.make_async_copy(early_ref.at[:base], total_ref.at[:base], early_sems.at[0]),
            pltpu.make_async_copy(early_ref.at[base:], total_ref.at[last:], early_sems.at[1]),
        ]
        for copy in copies:
            copy.start()
        total_ref[base:last] = jnp.zeros((full * size, total_ref.shape[1]), total_ref.dtype)
        for copy in copies:
            copy.wait()

    for to, rows, copies in chunks:
        for copy in copies:
            copy.wait()
        total_ref[base + rows.start : base + rows.stop] += lax.dot_general(
            rows_v[rows, to], train_v[:, to], (((1,), (1,)), ((), ())), preferred_element_type=jnp.float32)
    if finish is None:
        return

    f = lax.axis_index("feat")
    core, line = lax.rem(f, 2), f // 2
    lines, each = feats // 2, peers // feats
    for away in range(lines):
        to = lax.rem(line + away, lines) * 2
        for i in range(each):
            for ref, c in ((keep_ref, core), (give_ref, 1 - core)):
                row = rows_ref[0, (to + c) * each + i]
                block = total_ref[pl.ds(pl.multiple_of(jnp.maximum(row, 0) * size, size), size), :]
                ref[away * each + i] = jnp.where(row >= 0, block, 0.0)


def product(blocks, last, away, train, chain, finish=None):
    size = last[0].shape[0]
    examples, features = train.shape
    full, last_parts = len(blocks), sorted(away)
    operands = [*blocks, *(last if away else ()), *[a for h in last_parts for a in away[h]], train]
    count = (full + (PAIR if away else 0)) * size
    scratch = [
        pltpu.VMEM((count, features), train.dtype),
        pltpu.VMEM((examples, features), train.dtype),
        pltpu.SemaphoreType.DMA((features // math.gcd(features // 8, STEP), full + PAIR + 1)),
    ]
    in_specs = [ANY] * len(operands)
    if finish is None:
        out_shape, out_specs = jax.ShapeDtypeStruct((count, examples), jnp.float32), VMEM
        sizes = None
    else:
        peers, feats, early, rows = finish
        sizes = peers, feats
        operands += [early, rows]
        in_specs += [ANY, SMEM]
        out_shape = [jax.ShapeDtypeStruct((peers // 2, size, examples), jnp.float32)] * 2
        out_specs = [VMEM] * 2
        scratch = [
            pltpu.VMEM((len(slots_of(chain)) * PAIR * size, examples), jnp.float32),
            pltpu.SemaphoreType.DMA((2,)),
        ] + scratch
    return pl.pallas_call(
        functools.partial(product_kernel, chain, full, last_parts, sizes),
        in_specs=in_specs,
        out_specs=out_specs,
        out_shape=out_shape,
        scratch_shapes=scratch,
        cost_estimate=COST,
        compiler_params=pltpu.CompilerParams(vmem_limit_bytes=VMEM_LIMIT),
    )(*operands)


def shards(train_grads, audit_grads, owner_map, pair_blocks, pair_counts):
    peers, feats = lax.axis_size("ex"), lax.axis_size("feat")
    chain = peers // PAIR
    own = audit_grads[:, 0]
    parts = range(PARTS)
    across = [(i, i ^ 1) for i in range(peers)]
    upward = [(i, i + PAIR) for i in range(peers - PAIR)]
    downward = [(i + PAIR, i) for i in range(peers - PAIR)]

    half = cut(own)
    above, below = {(0, h): half[h] for h in parts}, {(0, h): half[h] for h in parts}

    def along(s, h):
        below[s, h] = lax.ppermute(below[s - 1, h], "ex", upward[(s - 1) * PAIR :])
        above[s, h] = lax.ppermute(above[s - 1, h], "ex", downward[: len(downward) - (s - 1) * PAIR])

    for h in parts:
        along(1, h)
    wanted, rows = plan(owner_map, pair_blocks, pair_counts, peers)
    asked = lax.ppermute(wanted, "ex", across)
    ends = [(i, i + PAIR) for i in range(PAIR)] + [(i, i - PAIR) for i in range(peers - PAIR, peers)]
    wants = jnp.concatenate([wanted, asked])
    notes = lax.ppermute(wants, "ex", ends)
    last = chain - 2

    slots = slots_of(chain)
    blocks = {}

    def hand_over(d):
        count = 1 + ((d, True) in slots)
        made = relay(wants, above, below, d, count, chain)
        for j in range(count):
            blocks[d, j > 0] = list(made[2 * j : 2 * j + 2])

    def receive(d, after=()):
        for second in (False, True):
            if (d, second) in slots:
                mine, theirs = blocks[d, second]
                if second:
                    theirs, blocks[d, False][1], after = lax.optimization_barrier((theirs, blocks[d, False][1], after))
                pairs = [(i, j) for i, j in across if not second or d <= i // PAIR < chain - d]
                blocks[d, second] = [mine, lax.ppermute(theirs, "ex", pairs)]

    hand_over(0)
    receive(0)
    hand_over(1)
    for s in range(2, chain - 1):
        for h in parts:
            if s == 2 and h == PARTS - 1:
                early = [slot for slot in slots if slot in blocks]
                gate = [blocks[slot][1] for slot in early]
                below[1, h], above[1, h], notes, gate = lax.optimization_barrier((below[1, h], above[1, h], notes, gate))
                for slot, block in zip(early, gate):
                    blocks[slot][1] = block
            along(s, h)

    straight = [(j, i) for i, j in ends]
    diagonal = [(j, i ^ 1) for i, j in ends]
    beyond = [(i, j) for i, j in across if not PAIR <= i < peers - PAIR]
    away = {}
    for h in parts:
        up, down = above[last, h], below[last, h]
        if h > 0:
            mine, theirs = away[h - 1]
            up, down, theirs = lax.optimization_barrier((up, down, theirs))
            away[h - 1] = mine, theirs
        mine, theirs = hand(notes, up, down, chain, False)
        if h == 0:
            receive(1, (mine, theirs))
        away[h] = lax.ppermute(mine, "ex", straight), lax.ppermute(theirs, "ex", diagonal)
    tail = {PARTS - 1: away.pop(PARTS - 1)}

    for d in range(2, chain - 1):
        hand_over(d)
        receive(d)

    def scores(group, away, finish=None):
        return product([b for s in group for b in blocks[s]], blocks[slots[-1]], away, train_grads, chain, finish)

    early = scores(slots[:2], away)
    keep, give = scores(slots[2:-1], tail, (peers, feats, early, rows))

    total = keep + lax.ppermute(give, "feat", [(i, i ^ 1) for i in range(feats)])
    lines, each = feats // 2, peers // feats
    result = total[:each]
    for away in range(1, lines):
        send = total[away * each : (away + 1) * each]
        result = result + lax.ppermute(send, "feat", [(i, (i + 2 * away) % feats) for i in range(feats)])
    return result[None]


def solution(mesh):
    in_specs = (P("ex", "feat"), P(None, "ex", None, "feat"), P(), P("ex", None), P("ex"))
    out_specs = P("ex", "feat", None, None)
    return jax.shard_map(shards, mesh=mesh, in_specs=in_specs, out_specs=out_specs, check_vma=False)
```

```python
import functools
import math

import jax
import jax.numpy as jnp
from jax import lax
from jax.experimental import pallas as pl
from jax.experimental.pallas import tpu as pltpu
from jax.sharding import PartitionSpec as P

PAIR = 2
PARTS = 2
EIGHTHS = 3
STEP = 1024
SMALL_LIMIT = 8 * 2**20
VMEM_LIMIT = 46 * 2**20
COST = pl.CostEstimate(flops=0, bytes_accessed=0, transcendentals=0)
SMEM = pl.BlockSpec(memory_space=pltpu.SMEM)
VMEM = pl.BlockSpec(memory_space=pltpu.VMEM)
ANY = pl.BlockSpec(memory_space=pl.ANY)


def cuts_of(features):
    return 0, features - features * EIGHTHS // 8, features


def slots_of(chain):
    first = [(d, False) for d in range(1, chain - 1)]
    return [(0, False)] + first + [(d, True) for d in range((chain - 1) // 2, 0, -1)]


def plan_kernel(peers, owner_ref, pairs_ref, counts_ref, wanted_ref, rows_ref):
    chain = peers // PAIR
    slots = len(slots_of(chain))
    me = lax.axis_index("ex")
    place, column = me // PAIR, lax.rem(me, PAIR)
    lane = lax.broadcasted_iota(jnp.int32, (1, peers), 1)
    wanted, rows = jnp.zeros((1, peers), jnp.int32), jnp.zeros((1, peers), jnp.int32)
    for k in range(peers):
        stored = owner_ref[pairs_ref[0, k]]
        holder = lax.rem(stored, peers)
        wanted = jnp.where(lane == holder, stored // peers, wanted)
        there = holder // PAIR
        far = jnp.abs(there - place)
        second = jnp.logical_and(there > place, place >= far)
        slot = jnp.where(far == chain - 1, slots - 1, jnp.where(second, slots - far, far))
        row = slot * PAIR + (lax.rem(holder, PAIR) != column).astype(jnp.int32)
        rows = jnp.where(lane == k, jnp.where(k < counts_ref[0], row, -1), rows)
    wanted_ref[...] = wanted
    rows_ref[...] = rows


def plan(owner_map, pair_blocks, pair_counts, peers):
    shape = jax.ShapeDtypeStruct((1, peers), jnp.int32)
    return pl.pallas_call(
        functools.partial(plan_kernel, peers), in_specs=[SMEM] * 3, out_specs=[VMEM] * 2, out_shape=[shape] * 2
    )(owner_map, pair_blocks, pair_counts)


def relay_kernel(chain, d, count, wants_ref, *refs):
    sources, outs, sems = refs[: -2 * count - 1], refs[-2 * count - 1 : -1], refs[-1]
    above_refs, below_refs = sources[:PARTS], sources[PARTS:]
    me = lax.axis_index("ex")
    place, column = me // PAIR, lax.rem(me, PAIR)

    def copies(j, blocks, source):
        made = []
        cuts = cuts_of(outs[0].shape[-1])
        for h, ref in enumerate(blocks):
            at = slice(cuts[h], cuts[h + 1])
            made += [
                pltpu.make_async_copy(ref.at[wants_ref[1, source]], outs[2 * j + 1].at[:, at], sems.at[j, 2 * h]),
                pltpu.make_async_copy(ref.at[wants_ref[0, source]], outs[2 * j].at[:, at], sems.at[j, 2 * h + 1]),
            ]
        return made

    up = copies(0, above_refs, jnp.minimum(place + d, chain - 1) * PAIR + column)
    waits = list(up)
    if below_refs:
        down = copies(0, below_refs, jnp.maximum(place - d, 0) * PAIR + column)

        @pl.when(place >= d)
        def _():
            for copy in down:
                copy.start()

        @pl.when(place < d)
        def _():
            for copy in up:
                copy.start()
    else:
        for copy in up:
            copy.start()
    if count > 1:
        waits += copies(1, above_refs, jnp.minimum(place + d, chain - 1) * PAIR + column)
        for copy in waits[len(up) :]:
            copy.start()
    for copy in waits:
        copy.wait()


def relay(wants, above, below, d, count, chain):
    blocks = [above[d, h] for h in range(PARTS)] + ([below[d, h] for h in range(PARTS)] if d else [])
    features = sum(b.shape[2] for b in blocks[:PARTS])
    shape = jax.ShapeDtypeStruct((blocks[0].shape[1], features), blocks[0].dtype)
    return pl.pallas_call(
        functools.partial(relay_kernel, chain, d, count),
        in_specs=[SMEM] + [ANY] * len(blocks),
        out_specs=[VMEM] * (2 * count),
        out_shape=[shape] * (2 * count),
        scratch_shapes=[pltpu.SemaphoreType.DMA((count, 2 * PARTS))],
        cost_estimate=COST,
        compiler_params=pltpu.CompilerParams(vmem_limit_bytes=SMALL_LIMIT),
    )(wants, *blocks)


def cut_kernel(own_ref, *refs):
    outs, sems = refs[:-1], refs[-1]
    cuts = cuts_of(own_ref.shape[-1])
    copies = [
        pltpu.make_async_copy(own_ref.at[:, :, cuts[h] : cuts[h + 1]], out, sems.at[h]) for h, out in enumerate(outs)
    ]
    for copy in copies:
        copy.start()
    for copy in copies:
        copy.wait()


def cut(own):
    cuts = cuts_of(own.shape[2])
    return pl.pallas_call(
        cut_kernel,
        in_specs=[ANY],
        out_specs=[VMEM] * PARTS,
        out_shape=[
            jax.ShapeDtypeStruct(own.shape[:2] + (stop - start,), own.dtype) for start, stop in zip(cuts, cuts[1:])
        ],
        scratch_shapes=[pltpu.SemaphoreType.DMA((PARTS,))],
        cost_estimate=COST,
        compiler_params=pltpu.CompilerParams(vmem_limit_bytes=VMEM_LIMIT),
    )(own)


def hand_kernel(chain, notes_ref, above_ref, below_ref, *refs):
    outs, sems = refs[:-1], refs[-1]
    outs = [outs[0].at[i] for i in range(PAIR)] if len(outs) == 1 else outs
    me = lax.axis_index("ex")
    place, column = me // PAIR, lax.rem(me, PAIR)
    for ref, source, upper in ((above_ref, (chain - 1) * PAIR + column, False), (below_ref, column, True)):

        @pl.when((place >= chain // 2) == upper)
        def _():
            copies = [
                pltpu.make_async_copy(ref.at[notes_ref[i, source]], out, sems.at[i]) for i, out in enumerate(outs)
            ]
            for copy in copies:
                copy.start()
            for copy in copies:
                copy.wait()


def hand(notes, above, below, chain, stacked):
    shape = above.shape[1:]
    return pl.pallas_call(
        functools.partial(hand_kernel, chain),
        in_specs=[SMEM] + [ANY] * 2,
        out_specs=VMEM if stacked else [VMEM] * PAIR,
        out_shape=jax.ShapeDtypeStruct((PAIR,) + shape, above.dtype)
        if stacked
        else [jax.ShapeDtypeStruct(shape, above.dtype)] * PAIR,
        scratch_shapes=[pltpu.SemaphoreType.DMA((PAIR,))],
        cost_estimate=COST,
        compiler_params=pltpu.CompilerParams(vmem_limit_bytes=SMALL_LIMIT),
    )(notes, above, below)


def product_kernel(chain, full, last_parts, finish, *refs):
    blocks, refs = refs[:full], refs[full:]
    near_refs, refs = (refs[:PAIR], refs[PAIR:]) if last_parts else ((), refs)
    away_refs, refs = refs[: PAIR * len(last_parts)], refs[PAIR * len(last_parts) :]
    train_ref, refs = refs[0], refs[1:]
    rows_v, train_v, sems = refs[-3:]
    size, features = (blocks or near_refs)[0].shape
    cuts = cuts_of(features)
    place = lax.axis_index("ex") // PAIR
    end = jnp.logical_or(place == 0, place == chain - 1)
    chunks, near, away, starts = [], [], [], []
    for h in range(PARTS):
        if not full and h not in last_parts:
            continue
        step = math.gcd(cuts[h + 1] - cuts[h], STEP)
        for at in range(cuts[h], cuts[h + 1], step):
            i = len(chunks)
            to = slice(at, at + step)

            def rows(b, source):
                return pltpu.make_async_copy(source, rows_v.at[b * size : (b + 1) * size, to], sems.at[i, b])

            copies = [pltpu.make_async_copy(train_ref.at[:, to], train_v.at[:, to], sems.at[i, full + PAIR])]
            copies += [rows(b, ref.at[:, to]) for b, ref in enumerate(blocks)]
            starts.append(list(copies))
            if h in last_parts:
                pair = away_refs[last_parts.index(h) * PAIR :][:PAIR]
                of_part = slice(at - cuts[h], at - cuts[h] + step)
                away.append([rows(full + b, ref.at[:, of_part]) for b, ref in enumerate(pair)])
                near.append([rows(full + b, ref.at[:, to]) for b, ref in enumerate(near_refs)])
                copies += near[-1]
            chunks.append((to, slice(0 if full else full * size, (full + PAIR * (h in last_parts)) * size), copies))

    @pl.when(end)
    def _():
        for copies in away:
            for copy in copies:
                copy.start()

    @pl.when(jnp.logical_not(end))
    def _():
        for copies in near:
            for copy in copies:
                copy.start()

    for copies in starts:
        for copy in copies:
            copy.start()

    if finish is None:
        total_ref, base = refs[0], 0
        total_ref[...] = jnp.zeros_like(total_ref)
    else:
        peers, feats, early = finish
        early_refs, (rows_ref, keep_ref, give_ref, total_ref, early_sems) = refs[:early], refs[early:-3]
        base = total_ref.shape[0] - PAIR * size
        copies, at = [], 0
        for i, ref in enumerate(early_refs):
            copies.append(pltpu.make_async_copy(ref, total_ref.at[at : at + ref.shape[0]], early_sems.at[i]))
            at += ref.shape[0]
        for copy in copies:
            copy.start()
        for copy in copies:
            copy.wait()

    for to, rows, copies in chunks:
        for copy in copies:
            copy.wait()
        total_ref[base + rows.start : base + rows.stop] += lax.dot_general(
            rows_v[rows, to], train_v[:, to], (((1,), (1,)), ((), ())), preferred_element_type=jnp.float32)
    if finish is None:
        return

    f = lax.axis_index("feat")
    core, line = lax.rem(f, 2), f // 2
    lines, each = feats // 2, peers // feats
    for away in range(lines):
        to = lax.rem(line + away, lines) * 2
        for i in range(each):
            for ref, c in ((keep_ref, core), (give_ref, 1 - core)):
                row = rows_ref[0, (to + c) * each + i]
                block = total_ref[pl.ds(pl.multiple_of(jnp.maximum(row, 0) * size, size), size), :]
                ref[away * each + i] = jnp.where(row >= 0, block, 0.0)


def product(blocks, last, away, train, chain, finish=None):
    size = last[0].shape[0]
    examples, features = train.shape
    full, last_parts = len(blocks), sorted(away)
    operands = [*blocks, *(last if away else ()), *[a for h in last_parts for a in away[h]], train]
    count = (full + (PAIR if away else 0)) * size
    scratch = [
        pltpu.VMEM((count, features), train.dtype),
        pltpu.VMEM((examples, features), train.dtype),
        pltpu.SemaphoreType.DMA((features // math.gcd(features // 8, STEP), full + PAIR + 1)),
    ]
    in_specs = [ANY] * len(operands)
    if finish is None:
        out_shape, out_specs = jax.ShapeDtypeStruct((count, examples), jnp.float32), VMEM
        sizes = None
    else:
        peers, feats, early, rows = finish
        sizes = peers, feats, len(early)
        operands += [*early, rows]
        in_specs += [ANY] * len(early) + [SMEM]
        out_shape = [jax.ShapeDtypeStruct((peers // 2, size, examples), jnp.float32)] * 2
        out_specs = [VMEM] * 2
        scratch = [
            pltpu.VMEM((len(slots_of(chain)) * PAIR * size, examples), jnp.float32),
            pltpu.SemaphoreType.DMA((len(early),)),
        ] + scratch
    return pl.pallas_call(
        functools.partial(product_kernel, chain, full, last_parts, sizes),
        in_specs=in_specs,
        out_specs=out_specs,
        out_shape=out_shape,
        scratch_shapes=scratch,
        cost_estimate=COST,
        compiler_params=pltpu.CompilerParams(vmem_limit_bytes=VMEM_LIMIT),
    )(*operands)


def shards(train_grads, audit_grads, owner_map, pair_blocks, pair_counts):
    peers, feats = lax.axis_size("ex"), lax.axis_size("feat")
    chain = peers // PAIR
    own = audit_grads[:, 0]
    parts = range(PARTS)
    across = [(i, i ^ 1) for i in range(peers)]
    upward = [(i, i + PAIR) for i in range(peers - PAIR)]
    downward = [(i + PAIR, i) for i in range(peers - PAIR)]

    half = cut(own)
    above, below = {(0, h): half[h] for h in parts}, {(0, h): half[h] for h in parts}

    def along(s, h):
        below[s, h] = lax.ppermute(below[s - 1, h], "ex", upward[(s - 1) * PAIR :])
        above[s, h] = lax.ppermute(above[s - 1, h], "ex", downward[: len(downward) - (s - 1) * PAIR])

    for h in parts:
        along(1, h)
    wanted, rows = plan(owner_map, pair_blocks, pair_counts, peers)
    asked = lax.ppermute(wanted, "ex", across)
    ends = [(i, i + PAIR) for i in range(PAIR)] + [(i, i - PAIR) for i in range(peers - PAIR, peers)]
    wants = jnp.concatenate([wanted, asked])
    notes = lax.ppermute(wants, "ex", ends)
    last = chain - 2

    slots = slots_of(chain)
    blocks = {}

    def hand_over(d):
        count = 1 + ((d, True) in slots)
        made = relay(wants, above, below, d, count, chain)
        for j in range(count):
            blocks[d, j > 0] = list(made[2 * j : 2 * j + 2])

    def receive(d, after=()):
        for second in (False, True):
            if (d, second) in slots:
                mine, theirs = blocks[d, second]
                if second:
                    theirs, blocks[d, False][1], after = lax.optimization_barrier((theirs, blocks[d, False][1], after))
                pairs = [(i, j) for i, j in across if not second or d <= i // PAIR < chain - d]
                blocks[d, second] = [mine, lax.ppermute(theirs, "ex", pairs)]

    hand_over(0)
    receive(0)
    hand_over(1)
    for s in range(2, chain - 1):
        for h in parts:
            if s == 2 and h == PARTS - 1:
                early = [slot for slot in slots if slot in blocks]
                gate = [blocks[slot][1] for slot in early]
                below[1, h], above[1, h], notes, gate = lax.optimization_barrier((below[1, h], above[1, h], notes, gate))
                for slot, block in zip(early, gate):
                    blocks[slot][1] = block
            along(s, h)

    straight = [(j, i) for i, j in ends]
    diagonal = [(j, i ^ 1) for i, j in ends]
    beyond = [(i, j) for i, j in across if not PAIR <= i < peers - PAIR]
    away = {}
    for h in parts:
        up, down = above[last, h], below[last, h]
        if h > 0:
            mine, theirs = away[h - 1]
            up, down, theirs = lax.optimization_barrier((up, down, theirs))
            away[h - 1] = mine, theirs
        mine, theirs = hand(notes, up, down, chain, False)
        if h == 0:
            receive(1)
        away[h] = lax.ppermute(mine, "ex", straight), lax.ppermute(theirs, "ex", diagonal)
    tail = {PARTS - 1: away.pop(PARTS - 1)}

    for d in range(2, chain - 1):
        hand_over(d)
        receive(d)

    def scores(group, away, finish=None):
        return product([b for s in group for b in blocks[s]], blocks[slots[-1]], away, train_grads, chain, finish)

    early = [scores(slots[:2], {}), scores(slots[2:-1], away)]
    keep, give = scores([], tail, (peers, feats, early, rows))

    total = keep + lax.ppermute(give, "feat", [(i, i ^ 1) for i in range(feats)])
    lines, each = feats // 2, peers // feats
    result = total[:each]
    for away in range(1, lines):
        send = total[away * each : (away + 1) * each]
        result = result + lax.ppermute(send, "feat", [(i, (i + 2 * away) % feats) for i in range(feats)])
    return result[None]


def solution(mesh):
    in_specs = (P("ex", "feat"), P(None, "ex", None, "feat"), P(), P("ex", None), P("ex"))
    out_specs = P("ex", "feat", None, None)
    return jax.shard_map(shards, mesh=mesh, in_specs=in_specs, out_specs=out_specs, check_vma=False)
```

```python
import functools
import math

import jax
import jax.numpy as jnp
from jax import lax
from jax.experimental import pallas as pl
from jax.experimental.pallas import tpu as pltpu
from jax.sharding import PartitionSpec as P

PAIR = 2
PARTS = 2
EIGHTHS = 3
STEP = 1024
SMALL_LIMIT = 8 * 2**20
VMEM_LIMIT = 46 * 2**20
COST = pl.CostEstimate(flops=0, bytes_accessed=0, transcendentals=0)
SMEM = pl.BlockSpec(memory_space=pltpu.SMEM)
VMEM = pl.BlockSpec(memory_space=pltpu.VMEM)
ANY = pl.BlockSpec(memory_space=pl.ANY)


def cuts_of(features):
    return 0, features - features * EIGHTHS // 8, features


def slots_of(chain):
    first = [(d, False) for d in range(1, chain - 1)]
    return [(0, False)] + first + [(d, True) for d in range((chain - 1) // 2, 0, -1)]


def plan_kernel(peers, owner_ref, pairs_ref, counts_ref, wanted_ref, rows_ref):
    chain = peers // PAIR
    slots = len(slots_of(chain))
    me = lax.axis_index("ex")
    place, column = me // PAIR, lax.rem(me, PAIR)
    lane = lax.broadcasted_iota(jnp.int32, (1, peers), 1)
    wanted, rows = jnp.zeros((1, peers), jnp.int32), jnp.zeros((1, peers), jnp.int32)
    for k in range(peers):
        stored = owner_ref[pairs_ref[0, k]]
        holder = lax.rem(stored, peers)
        wanted = jnp.where(lane == holder, stored // peers, wanted)
        there = holder // PAIR
        far = jnp.abs(there - place)
        second = jnp.logical_and(there > place, place >= far)
        slot = jnp.where(far == chain - 1, slots - 1, jnp.where(second, slots - far, far))
        row = slot * PAIR + (lax.rem(holder, PAIR) != column).astype(jnp.int32)
        rows = jnp.where(lane == k, jnp.where(k < counts_ref[0], row, -1), rows)
    wanted_ref[...] = wanted
    rows_ref[...] = rows


def plan(owner_map, pair_blocks, pair_counts, peers):
    shape = jax.ShapeDtypeStruct((1, peers), jnp.int32)
    return pl.pallas_call(
        functools.partial(plan_kernel, peers), in_specs=[SMEM] * 3, out_specs=[VMEM] * 2, out_shape=[shape] * 2
    )(owner_map, pair_blocks, pair_counts)


def relay_kernel(chain, d, count, wants_ref, *refs):
    sources, outs, sems = refs[: -2 * count - 1], refs[-2 * count - 1 : -1], refs[-1]
    above_refs, below_refs = sources[:PARTS], sources[PARTS:]
    me = lax.axis_index("ex")
    place, column = me // PAIR, lax.rem(me, PAIR)

    def copies(j, blocks, source):
        made = []
        cuts = cuts_of(outs[0].shape[-1])
        for h, ref in enumerate(blocks):
            at = slice(cuts[h], cuts[h + 1])
            made += [
                pltpu.make_async_copy(ref.at[wants_ref[1, source]], outs[2 * j + 1].at[:, at], sems.at[j, 2 * h]),
                pltpu.make_async_copy(ref.at[wants_ref[0, source]], outs[2 * j].at[:, at], sems.at[j, 2 * h + 1]),
            ]
        return made

    up = copies(0, above_refs, jnp.minimum(place + d, chain - 1) * PAIR + column)
    waits = list(up)
    if below_refs:
        down = copies(0, below_refs, jnp.maximum(place - d, 0) * PAIR + column)

        @pl.when(place >= d)
        def _():
            for copy in down:
                copy.start()

        @pl.when(place < d)
        def _():
            for copy in up:
                copy.start()
    else:
        for copy in up:
            copy.start()
    if count > 1:
        waits += copies(1, above_refs, jnp.minimum(place + d, chain - 1) * PAIR + column)
        for copy in waits[len(up) :]:
            copy.start()
    for copy in waits:
        copy.wait()


def relay(wants, above, below, d, count, chain):
    blocks = [above[d, h] for h in range(PARTS)] + ([below[d, h] for h in range(PARTS)] if d else [])
    features = sum(b.shape[2] for b in blocks[:PARTS])
    shape = jax.ShapeDtypeStruct((blocks[0].shape[1], features), blocks[0].dtype)
    return pl.pallas_call(
        functools.partial(relay_kernel, chain, d, count),
        in_specs=[SMEM] + [ANY] * len(blocks),
        out_specs=[VMEM] * (2 * count),
        out_shape=[shape] * (2 * count),
        scratch_shapes=[pltpu.SemaphoreType.DMA((count, 2 * PARTS))],
        cost_estimate=COST,
        compiler_params=pltpu.CompilerParams(vmem_limit_bytes=SMALL_LIMIT),
    )(wants, *blocks)


def cut_kernel(own_ref, *refs):
    outs, sems = refs[:-1], refs[-1]
    cuts = cuts_of(own_ref.shape[-1])
    copies = [
        pltpu.make_async_copy(own_ref.at[:, :, cuts[h] : cuts[h + 1]], out, sems.at[h]) for h, out in enumerate(outs)
    ]
    for copy in copies:
        copy.start()
    for copy in copies:
        copy.wait()


def cut(own):
    cuts = cuts_of(own.shape[2])
    return pl.pallas_call(
        cut_kernel,
        in_specs=[ANY],
        out_specs=[VMEM] * PARTS,
        out_shape=[
            jax.ShapeDtypeStruct(own.shape[:2] + (stop - start,), own.dtype) for start, stop in zip(cuts, cuts[1:])
        ],
        scratch_shapes=[pltpu.SemaphoreType.DMA((PARTS,))],
        cost_estimate=COST,
        compiler_params=pltpu.CompilerParams(vmem_limit_bytes=VMEM_LIMIT),
    )(own)


def hand_kernel(chain, notes_ref, above_ref, below_ref, *refs):
    outs, sems = refs[:-1], refs[-1]
    outs = [outs[0].at[i] for i in range(PAIR)] if len(outs) == 1 else outs
    me = lax.axis_index("ex")
    place, column = me // PAIR, lax.rem(me, PAIR)
    for ref, source, upper in ((above_ref, (chain - 1) * PAIR + column, False), (below_ref, column, True)):

        @pl.when((place >= chain // 2) == upper)
        def _():
            copies = [
                pltpu.make_async_copy(ref.at[notes_ref[i, source]], out, sems.at[i]) for i, out in enumerate(outs)
            ]
            for copy in copies:
                copy.start()
            for copy in copies:
                copy.wait()


def hand(notes, above, below, chain, stacked):
    shape = above.shape[1:]
    return pl.pallas_call(
        functools.partial(hand_kernel, chain),
        in_specs=[SMEM] + [ANY] * 2,
        out_specs=VMEM if stacked else [VMEM] * PAIR,
        out_shape=jax.ShapeDtypeStruct((PAIR,) + shape, above.dtype)
        if stacked
        else [jax.ShapeDtypeStruct(shape, above.dtype)] * PAIR,
        scratch_shapes=[pltpu.SemaphoreType.DMA((PAIR,))],
        cost_estimate=COST,
        compiler_params=pltpu.CompilerParams(vmem_limit_bytes=SMALL_LIMIT),
    )(notes, above, below)


def product_kernel(chain, full, last_parts, finish, *refs):
    blocks, refs = refs[:full], refs[full:]
    near_refs, refs = (refs[:PAIR], refs[PAIR:]) if last_parts else ((), refs)
    away_refs, refs = refs[: PAIR * len(last_parts)], refs[PAIR * len(last_parts) :]
    train_ref, refs = refs[0], refs[1:]
    rows_v, train_v, sems = refs[-3:]
    size, features = (blocks or near_refs)[0].shape
    cuts = cuts_of(features)
    place = lax.axis_index("ex") // PAIR
    end = jnp.logical_or(place == 0, place == chain - 1)
    chunks, near, away, starts = [], [], [], []
    for h in range(PARTS):
        if not full and h not in last_parts:
            continue
        step = math.gcd(cuts[h + 1] - cuts[h], STEP)
        for at in range(cuts[h], cuts[h + 1], step):
            i = len(chunks)
            to = slice(at, at + step)

            def rows(b, source):
                return pltpu.make_async_copy(source, rows_v.at[b * size : (b + 1) * size, to], sems.at[i, b])

            copies = [pltpu.make_async_copy(train_ref.at[:, to], train_v.at[:, to], sems.at[i, full + PAIR])]
            copies += [rows(b, ref.at[:, to]) for b, ref in enumerate(blocks)]
            starts.append(list(copies))
            if h in last_parts:
                pair = away_refs[last_parts.index(h) * PAIR :][:PAIR]
                of_part = slice(at - cuts[h], at - cuts[h] + step)
                away.append([rows(full + b, ref.at[:, of_part]) for b, ref in enumerate(pair)])
                near.append([rows(full + b, ref.at[:, to]) for b, ref in enumerate(near_refs)])
                copies += near[-1]
            chunks.append((to, slice(0 if full else full * size, (full + PAIR * (h in last_parts)) * size), copies))

    @pl.when(end)
    def _():
        for copies in away:
            for copy in copies:
                copy.start()

    @pl.when(jnp.logical_not(end))
    def _():
        for copies in near:
            for copy in copies:
                copy.start()

    for copies in starts:
        for copy in copies:
            copy.start()

    if finish is None:
        total_ref, base = refs[0], 0
        total_ref[...] = jnp.zeros_like(total_ref)
    else:
        peers, feats = finish
        early_ref, rows_ref, keep_ref, give_ref, total_ref, early_sems = refs[:-3]
        last = total_ref.shape[0] - PAIR * size
        base = last - full * size
        copies = [
            pltpu.make_async_copy(early_ref.at[:base], total_ref.at[:base], early_sems.at[0]),
            pltpu.make_async_copy(early_ref.at[base:], total_ref.at[last:], early_sems.at[1]),
        ]
        for copy in copies:
            copy.start()
        total_ref[base:last] = jnp.zeros((full * size, total_ref.shape[1]), total_ref.dtype)
        for copy in copies:
            copy.wait()

    for to, rows, copies in chunks:
        for copy in copies:
            copy.wait()
        total_ref[base + rows.start : base + rows.stop] += lax.dot_general(
            rows_v[rows, to], train_v[:, to], (((1,), (1,)), ((), ())), preferred_element_type=jnp.float32)
    if finish is None:
        return

    f = lax.axis_index("feat")
    core, line = lax.rem(f, 2), f // 2
    lines, each = feats // 2, peers // feats
    for away in range(lines):
        to = lax.rem(line + away, lines) * 2
        for i in range(each):
            for ref, c in ((keep_ref, core), (give_ref, 1 - core)):
                row = rows_ref[0, (to + c) * each + i]
                block = total_ref[pl.ds(pl.multiple_of(jnp.maximum(row, 0) * size, size), size), :]
                ref[away * each + i] = jnp.where(row >= 0, block, 0.0)


def product(blocks, last, away, train, chain, finish=None):
    size = last[0].shape[0]
    examples, features = train.shape
    full, last_parts = len(blocks), sorted(away)
    operands = [*blocks, *(last if away else ()), *[a for h in last_parts for a in away[h]], train]
    count = (full + (PAIR if away else 0)) * size
    scratch = [
        pltpu.VMEM((count, features), train.dtype),
        pltpu.VMEM((examples, features), train.dtype),
        pltpu.SemaphoreType.DMA((features // math.gcd(features // 8, STEP), full + PAIR + 1)),
    ]
    in_specs = [ANY] * len(operands)
    if finish is None:
        out_shape, out_specs = jax.ShapeDtypeStruct((count, examples), jnp.float32), VMEM
        sizes = None
    else:
        peers, feats, early, rows = finish
        sizes = peers, feats
        operands += [early, rows]
        in_specs += [ANY, SMEM]
        out_shape = [jax.ShapeDtypeStruct((peers // 2, size, examples), jnp.float32)] * 2
        out_specs = [VMEM] * 2
        scratch = [
            pltpu.VMEM((len(slots_of(chain)) * PAIR * size, examples), jnp.float32),
            pltpu.SemaphoreType.DMA((2,)),
        ] + scratch
    return pl.pallas_call(
        functools.partial(product_kernel, chain, full, last_parts, sizes),
        in_specs=in_specs,
        out_specs=out_specs,
        out_shape=out_shape,
        scratch_shapes=scratch,
        cost_estimate=COST,
        compiler_params=pltpu.CompilerParams(vmem_limit_bytes=VMEM_LIMIT),
    )(*operands)


def shards(train_grads, audit_grads, owner_map, pair_blocks, pair_counts):
    peers, feats = lax.axis_size("ex"), lax.axis_size("feat")
    chain = peers // PAIR
    own = audit_grads[:, 0]
    parts = range(PARTS)
    across = [(i, i ^ 1) for i in range(peers)]
    upward = [(i, i + PAIR) for i in range(peers - PAIR)]
    downward = [(i + PAIR, i) for i in range(peers - PAIR)]

    half = cut(own)
    above, below = {(0, h): half[h] for h in parts}, {(0, h): half[h] for h in parts}

    def along(s, h):
        below[s, h] = lax.ppermute(below[s - 1, h], "ex", upward[(s - 1) * PAIR :])
        above[s, h] = lax.ppermute(above[s - 1, h], "ex", downward[: len(downward) - (s - 1) * PAIR])

    for h in parts:
        along(1, h)
    wanted, rows = plan(owner_map, pair_blocks, pair_counts, peers)
    asked = lax.ppermute(wanted, "ex", across)
    ends = [(i, i + PAIR) for i in range(PAIR)] + [(i, i - PAIR) for i in range(peers - PAIR, peers)]
    wants = jnp.concatenate([wanted, asked])
    notes = lax.ppermute(wants, "ex", ends)
    last = chain - 2

    slots = slots_of(chain)
    blocks = {}

    def hand_over(d):
        count = 1 + ((d, True) in slots)
        made = relay(wants, above, below, d, count, chain)
        for j in range(count):
            blocks[d, j > 0] = list(made[2 * j : 2 * j + 2])

    def receive(d, after=()):
        for second in (False, True):
            if (d, second) in slots:
                mine, theirs = blocks[d, second]
                if second:
                    theirs, blocks[d, False][1], after = lax.optimization_barrier((theirs, blocks[d, False][1], after))
                pairs = [(i, j) for i, j in across if not second or d <= i // PAIR < chain - d]
                blocks[d, second] = [mine, lax.ppermute(theirs, "ex", pairs)]

    hand_over(0)
    receive(0)
    hand_over(1)
    for s in range(2, chain - 1):
        for h in parts:
            if s == 2 and h == PARTS - 1:
                early = [slot for slot in slots if slot in blocks]
                gate = [blocks[slot][1] for slot in early]
                below[1, h], above[1, h], notes, gate = lax.optimization_barrier((below[1, h], above[1, h], notes, gate))
                for slot, block in zip(early, gate):
                    blocks[slot][1] = block
            along(s, h)

    straight = [(j, i) for i, j in ends]
    diagonal = [(j, i ^ 1) for i, j in ends]
    beyond = [(i, j) for i, j in across if not PAIR <= i < peers - PAIR]
    away = {}
    for h in parts:
        up, down = above[last, h], below[last, h]
        if h > 0:
            mine, theirs = away[h - 1]
            up, down, theirs = lax.optimization_barrier((up, down, theirs))
            away[h - 1] = mine, theirs
        mine, theirs = hand(notes, up, down, chain, False)
        if h == 0:
            receive(1)
        away[h] = lax.ppermute(mine, "ex", straight), lax.ppermute(theirs, "ex", diagonal)
    tail = {PARTS - 1: away.pop(PARTS - 1)}

    for d in range(2, chain - 1):
        hand_over(d)
        receive(d)

    def scores(group, away, finish=None):
        return product([b for s in group for b in blocks[s]], blocks[slots[-1]], away, train_grads, chain, finish)

    early = scores(slots[:2], away)
    keep, give = scores(slots[2:-1], tail, (peers, feats, early, rows))

    total = keep + lax.ppermute(give, "feat", [(i, i ^ 1) for i in range(feats)])
    lines, each = feats // 2, peers // feats
    result = total[:each]
    for away in range(1, lines):
        send = total[away * each : (away + 1) * each]
        result = result + lax.ppermute(send, "feat", [(i, (i + 2 * away) % feats) for i in range(feats)])
    return result[None]


def solution(mesh):
    in_specs = (P("ex", "feat"), P(None, "ex", None, "feat"), P(), P("ex", None), P("ex"))
    out_specs = P("ex", "feat", None, None)
    return jax.shard_map(shards, mesh=mesh, in_specs=in_specs, out_specs=out_specs, check_vma=False)
```
